512 devices in a mesh: section: 8 (over z_lo, core), tensor: 16 (over y, z_hi), dp: 4 (over x).
Axes of the slice: x: 4, y: 4, z: 16 (z_hi: 4, z_lo: 4; z = z_hi * 4 + z_lo), core: 2. Of those that a mesh axis runs over, the one named last changes fastest.
Arguments:
- plan: int32 [8, 2], P('section'), may hold values from 0 to 1, each once within a row
- stashed: bfloat16 [8, 2, 1024, 8192], P('section', None, 'dp', 'tensor'), may hold values from -400 to 400
- norm_gain: bfloat16 [8, 8192], P('section', 'tensor'), may hold values from 0.099609375 to 1.8984375
- kv_weight: bfloat16 [8, 8192, 2048], P('section', 'tensor'), may hold values from -0.0625 to 0.0625
- kv_grad: bfloat16 [8, 2, 1024, 2048], P('section', None, ('dp', 'tensor')), may hold values from -4 to 4
- top_grad: bfloat16 [2, 1024, 8192], P(None, 'dp', 'tensor'), may hold values from -1.5 to 1.5
Outputs:
- input_grads: bfloat16 [8, 2, 1024, 8192], P('section', None, 'dp', 'tensor')
- weight_grads: bfloat16 [8, 8192, 2048], P('section', 'tensor', 'dp')
The draws below stay inside these ranges and needn't reach their ends.
Inputs may be any that keep to these rules, and one draw needn't show every extreme that they name: Each row of plan is a permutation of the micro-batch numbers.
All inputs are finite; a program needn't handle non-finite values.
Results may differ from the reference program's by a relative error of at most 0.0049.
Values may be sent and summed in bfloat16 or wider, within the bound.
No kernel may reach another device: no remote copies, remote signals or barrier semaphores. Data moves between devices by JAX's collectives and lax.ppermute only.
A program may use at most 64 MiB of HBM per device.

```python
import math
import jax
import jax.numpy as jnp
from jax import lax

D = 8192
KVW = 2048
MICRO = 2
SECTIONS = 8
TOKENS = 1024
N_DP = 4


def draw_stashed(key, part):
    key = jax.random.fold_in(key, 11)
    noise_key, col_key, row_key = jax.random.split(key, 3)
    full_shape = (SECTIONS, MICRO, TOKENS, D)
    col_scale = jnp.exp(jax.random.uniform(col_key, (D,), jnp.float32) * math.log(10.0))
    col_scale = col_scale * jnp.exp(jnp.arange(D, dtype=jnp.float32) * (math.log(3.0) / D))
    row_scale = jnp.exp(jax.random.uniform(row_key, (SECTIONS, MICRO, TOKENS, 1), jnp.float32) * math.log(10.0))
    values = jnp.clip(jax.random.normal(noise_key, full_shape, jnp.float32), -6.0, 6.0)
    return (0.2 * values * row_scale * col_scale).astype(jnp.bfloat16)


def raised(array, stream_key, source, target, parts, factor):
    def block_of(axis_at):
        return (jnp.arange(array.shape[axis_at]) // (array.shape[axis_at] // parts)).reshape((-1,) + (1,) * (array.ndim - 1 - axis_at))

    near = jax.random.permutation(stream_key, parts)[block_of(target)]
    far = (block_of(target) + parts // 2) % parts
    return jnp.where((block_of(source) == near) | (block_of(source) == far), factor * array, array)


def block_levels(stream_key, shape, shards, least, top_value):
    factor_of, own = 1.0, jax.random.fold_in(stream_key, 6)
    for axis_at, shards_of in shards:
        steps = jnp.exp(jax.random.uniform(jax.random.fold_in(own, axis_at), (shards_of,), jnp.float32, least / len(shards), top_value / len(shards)))
        factor_of = factor_of * jnp.repeat(steps, shape[axis_at] // shards_of).reshape([-1 if axis == axis_at else 1 for axis in range(len(shape))])
    return factor_of


def gaussian(key, shape, width, bound, pieces=(), held_as=jnp.bfloat16):
    array = jax.random.normal(key, shape, jnp.float32) * width
    if len(pieces) > 0:
        array = block_levels(key, shape, pieces, -0.22, 0.18) * array
    return jnp.clip(array, min=-bound, max=bound).astype(held_as)


def bell_draw_with(rng, shape, spread, most, pieces, heavy, kind=jnp.bfloat16):
    entries = spread * jax.random.normal(rng, shape, jnp.float32)
    if pieces:
        entries = entries * block_levels(rng, shape, pieces, -0.22, 0.18)
    return jnp.clip(raised(entries, jax.random.fold_in(rng, 3), *heavy), -most, most).astype(kind)


def setup_inputs(seed: int = 0) -> dict:
    keys = jax.random.split(jax.random.key(seed), 7)
    return {
        "plan": jax.vmap(lambda own: jax.random.permutation(own, MICRO))(jax.random.split(keys[0], SECTIONS)).reshape((SECTIONS, MICRO)).astype(jnp.int32),
        "stashed": draw_stashed(jax.random.fold_in(keys[6], 71), 0),
        "norm_gain": jnp.clip(1.0 + 0.18 * jax.random.normal(keys[2], (SECTIONS, D), jnp.float32), 0.099609375, 1.8984375).astype(jnp.bfloat16),
        "kv_weight": gaussian(keys[3], (SECTIONS, D, KVW), D ** -0.5, 0.0625, ((0, 8), (1, 16))),
        "kv_grad": bell_draw_with(keys[4], (SECTIONS, MICRO, TOKENS, KVW), 0.25, 4.0, ((0, 8), (2, 64)), (2, 3, 64, 4.0)),
        "top_grad": gaussian(keys[5], (MICRO, TOKENS, D), 0.25, 1.5, ((1, 4), (2, 16))),
    }


EPSILON = 1e-06

def section_terms(inputs):
    order_row, in_slots, gain_row, weight, grads = inputs
    slot_ids = jnp.arange(MICRO, dtype=jnp.int32)
    matches = order_row[None, :] == slot_ids[:, None]
    where_slot = lax.optimization_barrier(jnp.sum(jnp.where(matches, slot_ids[None, :], 0), axis=1)).astype(jnp.int32)
    hidden_in = jnp.take(in_slots, where_slot, axis=0).astype(jnp.float32)
    gains = gain_row.astype(jnp.float32)
    row_rms = jnp.sqrt(lax.optimization_barrier(jnp.sum(hidden_in * hidden_in, -1)) / D + EPSILON)
    normed = (gains * hidden_in / row_rms[..., None]).astype(jnp.bfloat16)
    flat_grads = grads.reshape(-1, KVW)
    normed_grad = jnp.dot(flat_grads, weight.T, preferred_element_type=jnp.float32).reshape(MICRO, TOKENS, D)
    aligned = lax.optimization_barrier(jnp.sum(gains * normed_grad * hidden_in, -1))
    contrib = gains * normed_grad / row_rms[..., None] - hidden_in * (aligned / (D * row_rms ** 3))[..., None]
    weight_grad = jnp.dot(normed.reshape(-1, D).T, flat_grads, preferred_element_type=jnp.float32)
    weight_grad = weight_grad / (MICRO * N_DP)
    return (contrib, weight_grad.astype(jnp.bfloat16))

def reference(plan, stashed, norm_gain, kv_weight, kv_grad, top_grad):
    contrib, weight_grads = lax.map(section_terms, (plan, stashed, norm_gain, kv_weight, kv_grad))
    from_above = jnp.cumsum(contrib[::-1], axis=0)[::-1]
    input_grads = (top_grad.astype(jnp.float32)[None] + from_above).astype(jnp.bfloat16)
    return (input_grads, weight_grads)
```

```python
import jax
import jax.numpy as jnp
from jax import lax
from jax.sharding import PartitionSpec as P

EPSILON = 1e-06
NY, NZ = 4, 4


def y_groups():
    return [[y * NZ + z for y in range(NY)] for z in range(NZ)]


def z_groups():
    return [[y * NZ + z for z in range(NZ)] for y in range(NY)]


def from_z(value, step):
    perm = [(y * NZ + (z + step) % NZ, y * NZ + z) for y in range(NY) for z in range(NZ)]
    return lax.ppermute(value, "tensor", perm)


def from_other_core(value):
    return lax.ppermute(value, "section", [(s, s ^ 1) for s in range(8)])


def from_chips_above(value, chips):
    return lax.ppermute(value, "section", [(s, s - 2 * chips) for s in range(2 * chips, 8)])


def to_all(value, axis, groups, count):
    spread = jnp.broadcast_to(value, (count,) + value.shape)
    return lax.all_to_all(spread, axis, 0, 0, axis_index_groups=groups)


def tensor_sum(value):
    value = jnp.sum(to_all(value, "tensor", y_groups(), NY), axis=0)
    return jnp.sum(to_all(value, "tensor", z_groups(), NZ), axis=0)


def shards(plan, stashed, norm_gain, kv_weight, kv_grad, top_grad):
    section = lax.axis_index("section")
    core = section % 2
    tz = lax.axis_index("tensor") % NZ
    width = stashed.shape[-1]
    model_width = lax.axis_size("tensor") * width
    data_count = lax.axis_size("dp")
    micro_count = plan.shape[1]
    rows = kv_grad.shape[2]
    tokens = micro_count * NY * NZ * rows

    def roll_z(value, by):
        return lax.dynamic_slice_in_dim(jnp.concatenate([value, value], axis=1), by % NZ, NZ, axis=1)

    def turned(value):
        value = value.reshape(micro_count, NY, NZ, rows, width).transpose(1, 2, 0, 3, 4)
        return roll_z(value, tz).reshape(tokens, width)

    def absolute(value):
        return roll_z(value.reshape(NY, NZ, -1), NZ - tz).reshape(-1, 128)

    def relative(value):
        return roll_z(value.reshape(NY, NZ, -1), tz).reshape(tokens)

    kv0 = kv_grad[0]
    z_parts = [from_z(kv0, d) for d in (1, 2, 3)]
    kv_own = to_all(kv0, "tensor", y_groups(), NY)
    kv_others = to_all(jnp.stack(z_parts), "tensor", y_groups(), NY)

    slots = jnp.where(plan[0, 0] == 0, stashed[0], stashed[0][::-1])
    hidden16 = turned(slots)
    hidden_all = lax.all_gather(hidden16, "section")
    hidden = hidden16.astype(jnp.float32)
    top = turned(top_grad)
    gains = norm_gain[0].astype(jnp.float32)
    squares = tensor_sum(absolute(jnp.sum(hidden * hidden, -1)))
    row_rms = jnp.sqrt(relative(squares) / model_width + EPSILON)
    normed = (gains * hidden / row_rms[:, None]).astype(jnp.bfloat16)

    def split(value):
        value = value.reshape((NY, NZ, micro_count * rows) + value.shape[1:])
        return value[:, :1], value[:, 1:]

    weight = kv_weight[0]
    flat_own = kv_own.reshape(-1, kv_own.shape[-1])
    flat_others = kv_others.reshape(-1, kv_own.shape[-1])

    def back(flat):
        product = lax.dot_general(
            flat, weight, (((1,), (1,)), ((), ())), preferred_element_type=jnp.float32
        )
        return product.reshape(NY, -1, micro_count * rows, width)

    normed_grad = jnp.concatenate([back(flat_own), back(flat_others)], axis=1).reshape(tokens, width)
    gained = gains * normed_grad
    aligned_part = jnp.sum(gained * hidden, -1)
    direct = gained / row_rms[:, None]
    direct16 = direct.astype(jnp.bfloat16)

    other = from_other_core(direct16).astype(jnp.float32)
    halves = (direct + other).reshape(2, tokens // 2, width)
    half = lax.dynamic_index_in_dim(halves, core, 0, keepdims=False).astype(jnp.bfloat16)
    above = sum(from_chips_above(half, d).astype(jnp.float32) for d in (1, 2, 3))
    above_other = from_other_core(above.astype(jnp.bfloat16)).astype(jnp.float32)
    first = core == 0
    above_all = jnp.concatenate([jnp.where(first, above, above_other), jnp.where(first, above_other, above)])

    aligned = relative(tensor_sum(absolute(aligned_part)))
    scale = (aligned / (model_width * row_rms**3)).reshape(-1, 128)
    scales = to_all(scale, "section", None, 8).reshape(8, tokens)
    later = jnp.arange(8)[:, None] >= section
    scales = jnp.where(later, scales, 0.0)
    correction = jnp.sum(hidden_all.astype(jnp.float32) * scales[:, :, None], axis=0)
    total = top.astype(jnp.float32) + direct + jnp.where(first, other, 0.0) + above_all - correction
    out = roll_z(total.astype(jnp.bfloat16).reshape(NY, NZ, micro_count, rows, width), NZ - tz)
    input_grads = out.transpose(2, 0, 1, 3, 4).reshape(1, micro_count, NY * NZ * rows, width)

    normed_own, normed_others = split(normed)

    def outer(left, right):
        return lax.dot_general(
            left.reshape(-1, width), right, (((0,), (0,)), ((), ())), preferred_element_type=jnp.float32
        )

    local_weight = outer(normed_own, flat_own) + outer(normed_others, flat_others)
    pieces = local_weight.astype(jnp.bfloat16).reshape(width, data_count, -1).transpose(1, 0, 2)
    got = lax.all_to_all(pieces, "dp", 0, 0)
    summed = jnp.sum(got.astype(jnp.float32), axis=0)
    weight_grads = (summed / (micro_count * data_count)).astype(jnp.bfloat16)[None]
    return (input_grads, weight_grads)


def solution(mesh):
    in_specs = (
        P("section", None),
        P("section", None, "dp", "tensor"),
        P("section", "tensor"),
        P("section", "tensor", None),
        P("section", None, ("dp", "tensor"), None),
        P(None, "dp", "tensor"),
    )
    out_specs = (P("section", None, "dp", "tensor"), P("section", "tensor", "dp"))
    return jax.shard_map(shards, mesh=mesh, in_specs=in_specs, out_specs=out_specs, check_vma=False)
```

```python
import jax
import jax.numpy as jnp
from jax import lax
from jax.sharding import PartitionSpec as P

EPSILON = 1e-06
NY, NZ = 4, 4


def y_groups():
    return [[y * NZ + z for y in range(NY)] for z in range(NZ)]


def z_groups():
    return [[y * NZ + z for z in range(NZ)] for y in range(NY)]


def from_z(value, step):
    perm = [(y * NZ + (z + step) % NZ, y * NZ + z) for y in range(NY) for z in range(NZ)]
    return lax.ppermute(value, "tensor", perm)


def from_y(value, step):
    perm = [((y + step) % NY * NZ + z, y * NZ + z) for y in range(NY) for z in range(NZ)]
    return lax.ppermute(value, "tensor", perm)


def from_x(value, step):
    return lax.ppermute(value, "dp", [((x + step) % 4, x) for x in range(4)])


def from_other_core(value):
    return lax.ppermute(value, "section", [(s, s ^ 1) for s in range(8)])


def from_chips_above(value, chips):
    return lax.ppermute(value, "section", [(s, s - 2 * chips) for s in range(2 * chips, 8)])


def to_all(value, axis, groups, count):
    spread = jnp.broadcast_to(value, (count,) + value.shape)
    return lax.all_to_all(spread, axis, 0, 0, axis_index_groups=groups)


def y_sum(value):
    return jnp.sum(to_all(value, "tensor", y_groups(), NY), axis=0)


def z_sum(value):
    return jnp.sum(to_all(value, "tensor", z_groups(), NZ), axis=0)


def shards(plan, stashed, norm_gain, kv_weight, kv_grad, top_grad):
    section = lax.axis_index("section")
    core = section % 2
    tz = lax.axis_index("tensor") % NZ
    ty = lax.axis_index("tensor") // NZ
    tx = lax.axis_index("dp")
    width = stashed.shape[-1]
    model_width = lax.axis_size("tensor") * width
    data_count = lax.axis_size("dp")
    micro_count = plan.shape[1]
    rows = kv_grad.shape[2]
    tokens = micro_count * NY * NZ * rows

    def roll_z(value, by):
        return lax.dynamic_slice_in_dim(jnp.concatenate([value, value], axis=1), by % NZ, NZ, axis=1)

    def turned(value):
        value = value.reshape(micro_count, NY, NZ, rows, width).transpose(1, 2, 0, 3, 4)
        return roll_z(value, tz).reshape(tokens, width)

    def absolute(value):
        return roll_z(value.reshape(NY, NZ, -1), NZ - tz).reshape(-1, 128)

    def relative(value):
        return roll_z(value.reshape(NY, NZ, -1), tz).reshape(tokens)

    kv0 = kv_grad[0]
    raw_all = lax.all_gather(stashed[0], "section")
    spread = jnp.broadcast_to(kv0, (NZ,) + kv0.shape)
    spread, kv_y = lax.optimization_barrier((spread, kv0))
    kv_z = lax.all_to_all(spread, "tensor", 0, 0, axis_index_groups=z_groups())
    y_parts = [from_y(kv_y, d) for d in (1, 2, 3)]
    kv_own = jnp.stack([kv_y] + y_parts)
    kv_own = lax.dynamic_slice_in_dim(jnp.concatenate([kv_own, kv_own]), NY - ty, NY)
    slots = jnp.where(plan[0, 0] == 0, stashed[0], stashed[0][::-1])
    hidden16 = turned(slots)
    hidden = hidden16.astype(jnp.float32)
    squares = absolute(jnp.sum(hidden * hidden, -1))
    squares, _ = lax.optimization_barrier((squares, y_parts[0]))
    squares = squares + sum(from_y(squares, d) for d in (1, 2, 3))
    kv_z, kv_own, squares = lax.optimization_barrier((kv_z, kv_own, squares))
    others = lax.dynamic_slice_in_dim(jnp.concatenate([kv_z, kv_z]), tz + 1, NZ - 1)
    kv_others = to_all(others, "tensor", y_groups(), NY)
    squares = squares + sum(from_z(squares, d) for d in (1, 3, 2))
    gains = norm_gain[0].astype(jnp.float32)
    row_rms = jnp.sqrt(relative(squares) / model_width + EPSILON)
    normed = (gains * hidden / row_rms[:, None]).astype(jnp.bfloat16)
    kv_others, normed, row_rms = lax.optimization_barrier((kv_others, normed, row_rms))

    def split(value):
        value = value.reshape((NY, NZ, micro_count * rows) + value.shape[1:])
        return value[:, :1], value[:, 1:]

    weight = kv_weight[0]
    flat_own = kv_own.reshape(-1, kv_own.shape[-1])
    flat_others = kv_others.reshape(-1, kv_own.shape[-1])

    def back(flat):
        product = lax.dot_general(
            flat, weight, (((1,), (1,)), ((), ())), preferred_element_type=jnp.float32
        )
        return product.reshape(NY, -1, micro_count * rows, width)

    normed_grad = jnp.concatenate([back(flat_own), back(flat_others)], axis=1).reshape(tokens, width)
    gained = gains * normed_grad
    aligned_part = jnp.sum(gained * hidden, -1)
    direct = gained / row_rms[:, None]
    direct16 = direct.astype(jnp.bfloat16)

    other = from_other_core(direct16)
    aligned_y = y_sum(absolute(aligned_part))
    other, aligned_y = lax.optimization_barrier((other, aligned_y))
    other = other.astype(jnp.float32)
    halves = (direct + other).reshape(2, tokens // 2, width)
    half = lax.dynamic_index_in_dim(halves, core, 0, keepdims=False).astype(jnp.bfloat16)
    normed, half = lax.optimization_barrier((normed, half))
    above = sum(from_chips_above(half, d).astype(jnp.float32) for d in (1, 2, 3))
    above_other = from_other_core(above.astype(jnp.bfloat16)).astype(jnp.float32)
    first = core == 0
    above_all = jnp.concatenate([jnp.where(first, above, above_other), jnp.where(first, above_other, above)])

    aligned = relative(z_sum(aligned_y))
    scale = (aligned / (model_width * row_rms**3)).reshape(-1, 128)
    swap = jnp.broadcast_to(plan[0, 0].astype(jnp.float32), (1, 128))
    scales = to_all(jnp.concatenate([scale, swap]), "section", None, 8)
    swaps = scales[:, -1, :1]
    scales = scales[:, :-1].reshape(8, tokens)
    later = jnp.arange(8)[:, None] >= section
    scales = jnp.where(later, scales, 0.0)
    ordered = jnp.where(swaps[:, :, None, None] == 0, raw_all, raw_all[:, ::-1])
    flat = scales.reshape(8, NY, NZ, micro_count, rows)
    flat = jax.vmap(lambda v: roll_z(v, NZ - tz))(flat).transpose(0, 3, 1, 2, 4).reshape(8, micro_count, -1)
    correction = jnp.sum(ordered.astype(jnp.float32) * flat[..., None], axis=0)
    total = direct + jnp.where(first, other, 0.0) + above_all
    total = roll_z(total.reshape(NY, NZ, micro_count, rows, width), NZ - tz)
    total = total.transpose(2, 0, 1, 3, 4).reshape(micro_count, NY * NZ * rows, width)
    input_grads = (top_grad.astype(jnp.float32) + total - correction).astype(jnp.bfloat16)[None]

    normed_own, normed_others = split(normed)

    def outer(left, right):
        return lax.dot_general(
            left.reshape(-1, width), right, (((0,), (0,)), ((), ())), preferred_element_type=jnp.float32
        )

    local_weight = outer(normed_own, flat_own) + outer(normed_others, flat_others)
    own_piece = lax.dynamic_slice_in_dim(local_weight, tx * width, width, axis=1)
    sent = local_weight.astype(jnp.bfloat16)

    def piece(step):
        at = (tx + 4 - step) % 4
        return lax.dynamic_slice_in_dim(sent, at * width, width, axis=1)

    summed = own_piece + sum(from_x(piece(d), d).astype(jnp.float32) for d in (1, 2, 3))
    weight_grads = (summed / (micro_count * data_count)).astype(jnp.bfloat16)[None]
    return (input_grads, weight_grads)


def solution(mesh):
    in_specs = (
        P("section", None),
        P("section", None, "dp", "tensor"),
        P("section", "tensor"),
        P("section", "tensor", None),
        P("section", None, ("dp", "tensor"), None),
        P(None, "dp", "tensor"),
    )
    out_specs = (P("section", None, "dp", "tensor"), P("section", "tensor", "dp"))
    return jax.shard_map(shards, mesh=mesh, in_specs=in_specs, out_specs=out_specs, check_vma=False)
```

```python
import functools

import jax
import jax.numpy as jnp
from jax import lax
from jax.experimental import pallas as pl
from jax.experimental.pallas import tpu as pltpu
from jax.sharding import PartitionSpec as P

EPSILON = 1e-06
NY, NZ, NX, NS = 4, 4, 4, 8
MICRO, ROWS, LANES = 2, 16, 128
BLOCKS = NY * NZ
F32, BF16 = jnp.float32, jnp.bfloat16
VMEM = pl.BlockSpec(memory_space=pltpu.VMEM)
SMEM = pl.BlockSpec(memory_space=pltpu.SMEM)


def y_groups():
    return [[y * NZ + z for y in range(NY)] for z in range(NZ)]


def z_groups():
    return [[y * NZ + z for z in range(NZ)] for y in range(NY)]


def from_y(value, step):
    perm = [((y + step) % NY * NZ + z, y * NZ + z) for y in range(NY) for z in range(NZ)]
    return lax.ppermute(value, "tensor", perm)


def from_z(value, step):
    perm = [(y * NZ + (z + step) % NZ, y * NZ + z) for y in range(NY) for z in range(NZ)]
    return lax.ppermute(value, "tensor", perm)


def from_x(value, step):
    return lax.ppermute(value, "dp", [((x + step) % NX, x) for x in range(NX)])


def from_other_core(value):
    return lax.ppermute(value, "section", [(s, s ^ 1) for s in range(NS)])


def from_chips_above(value, chips):
    return lax.ppermute(value, "section", [(s, s - 2 * chips) for s in range(2 * chips, NS)])


def y_exchange(spread):
    return lax.all_to_all(spread, "tensor", 0, 0, axis_index_groups=y_groups())


def z_exchange(spread):
    return lax.all_to_all(spread, "tensor", 0, 0, axis_index_groups=z_groups())


def call(body, out_shape, specs, args, scratch=(), cost=None):
    return pl.pallas_call(
        body,
        out_shape=out_shape,
        in_specs=specs,
        out_specs=jax.tree.map(lambda _: VMEM, out_shape),
        scratch_shapes=list(scratch),
        compiler_params=pltpu.CompilerParams(vmem_limit_bytes=28 * 2**20),
        cost_estimate=cost,
    )(*args)


def columns(row, count):
    return jnp.transpose(jnp.broadcast_to(row, (LANES, LANES)))[:, :1] + jnp.zeros((LANES, count), F32)


def spread_body(place, kv_ref, out_ref):
    for step in range(1, NZ):
        block = kv_ref[lax.rem(place[0] + step, NZ)]
        for y in range(NY):
            out_ref[y, step - 1] = block


def back_body(place, own0, own1, own2, own3, others, weight, gains, stashed, squares, direct, direct16, aligned, grad):
    tz, ty, swap = place[0], place[1], place[2]
    kvw = weight.shape[1]
    width = weight.shape[0]
    model_width = width * BLOCKS
    dims = (((1,), (1,)), ((), ()))

    def put(product, blocks):
        for at, (y, step) in enumerate(blocks):
            for m in range(MICRO):
                row = (at * MICRO + m) * ROWS
                grad[m, y * NZ + lax.rem(tz + step, NZ)] = product[row : row + ROWS]

    mine = jnp.concatenate([ref[...].reshape(MICRO * ROWS, kvw) for ref in (own0, own1, own2, own3)])
    product = lax.dot_general(mine, weight[...], dims, preferred_element_type=F32)
    put(product, [(lax.rem(ty + k, NY), 0) for k in range(NY)])
    for y in range(NY):
        rest = others[y].reshape((NZ - 1) * MICRO * ROWS, kvw)
        product = lax.dot_general(rest, weight[...], dims, preferred_element_type=F32)
        put(product, [(y, step) for step in range(1, NZ)])
    gain = gains[...].astype(F32)
    per = LANES // ROWS
    for chunk in range(MICRO * BLOCKS // per):
        m, first = chunk * per // BLOCKS, chunk * per % BLOCKS
        gained = grad[m, first : first + per].reshape(LANES, width) * gain
        hidden = stashed[m ^ swap, first * ROWS : (first + per) * ROWS].astype(F32)
        inverse = 1.0 / jnp.sqrt(squares[chunk : chunk + 1] / model_width + EPSILON)
        here = gained * columns(inverse, width)
        direct[chunk * LANES : (chunk + 1) * LANES] = here
        direct16[chunk * LANES : (chunk + 1) * LANES] = here.astype(BF16)
        terms = gained * hidden
        folded = sum(terms[:, k * LANES : (k + 1) * LANES] for k in range(width // LANES))
        total = jnp.sum(jnp.transpose(folded), axis=0, keepdims=True)
        for y in range(NY):
            aligned[y, chunk : chunk + 1] = total


def half_body(place, direct, other, out_ref):
    rows = out_ref.shape[0]
    at = pl.ds(pl.multiple_of(place[3] * rows, rows), rows)
    out_ref[...] = (direct[at] + other[at].astype(F32)).astype(BF16)


def outer_body(place, own0, own1, own2, own3, others, gains, stashed, squares, kept, sent1, sent2, sent3, normed, left):
    tz, ty, swap, tx = place[0], place[1], place[2], place[4]
    width = kept.shape[0]
    model_width = width * BLOCKS
    gain = gains[...].astype(F32)
    per = LANES // ROWS
    for chunk in range(MICRO * BLOCKS // per):
        m, first = chunk * per // BLOCKS, chunk * per % BLOCKS
        hidden = stashed[m ^ swap, first * ROWS : (first + per) * ROWS].astype(F32)
        inverse = 1.0 / jnp.sqrt(squares[chunk : chunk + 1] / model_width + EPSILON)
        here = gain * hidden * columns(inverse, width)
        normed[m, first : first + per] = here.astype(BF16).reshape(per, ROWS, width)
    blocks = [(lax.rem(ty + k, NY), 0) for k in range(NY)]
    blocks += [(y, step) for y in range(NY) for step in range(1, NZ)]
    for at, (y, step) in enumerate(blocks):
        for m in range(MICRO):
            row = (at * MICRO + m) * ROWS
            left[row : row + ROWS] = normed[m, y * NZ + lax.rem(tz + step, NZ)]
    turned = jnp.transpose(left[...])
    share = MICRO * ROWS
    for step, out_ref in enumerate((kept, sent1, sent2, sent3)):
        at = pl.ds(pl.multiple_of(lax.rem(tx + NX - step, NX) * width, width), width)
        mine = [ref[:, :, at].reshape(share, width) for ref in (own0, own1, own2, own3)]
        rest = others[:, :, :, :, at].reshape(NY * (NZ - 1) * share, width)
        right = jnp.concatenate(mine + [rest])
        out_ref[...] = jnp.dot(turned, right, preferred_element_type=F32).astype(out_ref.dtype)


def scale_body(place, parts, squares, out_ref, *, model_width):
    mean = squares[...] / model_width + EPSILON
    total = parts[0] + parts[1] + parts[2] + parts[3]
    scale = total / (model_width * (mean * jnp.sqrt(mean)))
    swap = jnp.full((NS - MICRO * BLOCKS * ROWS // LANES, LANES), place[2], jnp.int32).astype(F32)
    value = jnp.concatenate([scale, swap])
    for section in range(NS):
        out_ref[section] = value


def total_body(place, raw, scales, direct, other, above, above_other, top, out_ref):
    section, core = place[5], place[3]
    rows, width = raw.shape[2], raw.shape[3]
    chunk = pl.program_id(0)
    use_other = jnp.where(core == 0, 1.0, 0.0)
    fixes = [jnp.zeros((rows, width), F32) for _ in range(MICRO)]
    turned = []
    for m in range(MICRO):
        row = m * (BLOCKS * ROWS // LANES) + chunk
        turned.append(jnp.transpose(scales[:, pl.ds(row, 1)].reshape(NS, LANES)))
    for u in range(NS):
        live = jnp.where(u >= section, 1.0, 0.0)
        swapped = scales[u, NS - 1 : NS, :1] != 0.0
        slots = [raw[u, k].astype(F32) for k in range(MICRO)]
        for m in range(MICRO):
            hidden = jnp.where(swapped, slots[1 - m], slots[m])
            fixes[m] = fixes[m] + hidden * (turned[m][:, u : u + 1] * live)
    for m in range(MICRO):
        mine = jnp.where(core == m, above[...], above_other[...].astype(F32))
        value = top[m].astype(F32) + direct[m] + use_other * other[m].astype(F32) + mine - fixes[m]
        out_ref[m] = value.astype(BF16)


def shards(plan, stashed, norm_gain, kv_weight, kv_grad, top_grad):
    section = lax.axis_index("section")
    core = section % 2
    index = lax.axis_index("tensor")
    tz, ty, tx = index % NZ, index // NZ, lax.axis_index("dp")
    width = stashed.shape[-1]
    tokens = MICRO * BLOCKS * ROWS
    model_width = width * BLOCKS
    lines = tokens // LANES
    place = jnp.stack([tz, ty, plan[0, 0], core, tx, section]).astype(jnp.int32)
    kv0, slots, weight = kv_grad[0], stashed[0], kv_weight[0]
    kvw = kv0.shape[-1]
    half = (tokens // 2, width)

    spread = jnp.broadcast_to(kv0, (NZ,) + kv0.shape)
    spread, kv_y = lax.optimization_barrier((spread, kv0))
    kv_z = z_exchange(spread)
    own = [kv_y] + [from_y(kv_y, d) for d in (1, 2, 3)]
    squares = jnp.sum(jnp.square(slots.astype(F32)), -1).reshape(MICRO, lines // MICRO, LANES)
    squares = jnp.where(plan[0, 0] == 0, squares, squares[::-1]).reshape(lines, LANES)
    squares, _ = lax.optimization_barrier((squares, own[1]))
    squares = squares + sum(from_y(squares, d) for d in (1, 2, 3))
    kv_z, own, squares, slots_later = lax.optimization_barrier((kv_z, own, squares, slots))

    raw_all = lax.all_gather(slots_later, "section")
    shape = jax.ShapeDtypeStruct((NY, NZ - 1) + kv0.shape, BF16)
    others = y_exchange(call(spread_body, shape, [SMEM, VMEM], (place, kv_z)))
    squares = squares + sum(from_z(squares, d) for d in (1, 3, 2))
    others, squares = lax.optimization_barrier((others, squares))

    flops = 2 * tokens * width * kvw
    direct, direct16, aligned = call(
        back_body,
        (
            jax.ShapeDtypeStruct((tokens, width), F32),
            jax.ShapeDtypeStruct((tokens, width), BF16),
            jax.ShapeDtypeStruct((NY, lines, LANES), F32),
        ),
        [SMEM] + [VMEM] * 9,
        (place, *own, others, weight, norm_gain, slots, squares),
        [pltpu.VMEM((MICRO, BLOCKS, ROWS, width), F32)],
        pl.CostEstimate(flops=flops, bytes_accessed=6 * 2**20, transcendentals=0),
    )
    other = from_other_core(direct16)
    aligned = y_exchange(aligned)
    other, aligned = lax.optimization_barrier((other, aligned))
    aligned = jnp.sum(aligned, axis=0)

    chip = call(half_body, jax.ShapeDtypeStruct(half, BF16), [SMEM, VMEM, VMEM], (place, direct, other))
    above = sum(from_chips_above(chip, d).astype(F32) for d in (1, 2, 3))
    above_other = from_other_core(above.astype(BF16))

    aligned, own, others, _ = lax.optimization_barrier((aligned, own, others, chip))
    piece = jax.ShapeDtypeStruct((width, width), BF16)
    kept, *sent = call(
        outer_body,
        (jax.ShapeDtypeStruct((width, width), F32), piece, piece, piece),
        [SMEM] + [VMEM] * 8,
        (place, *own, others, norm_gain, slots, squares),
        [pltpu.VMEM((MICRO, BLOCKS, ROWS, width), BF16), pltpu.VMEM((tokens, width), BF16)],
        pl.CostEstimate(flops=flops, bytes_accessed=6 * 2**20, transcendentals=0),
    )
    summed = kept + sum(from_x(sent[d - 1], d).astype(F32) for d in (1, 2, 3))
    weight_grads = (summed / (MICRO * NX)).astype(BF16)[None]

    parts = z_exchange(jnp.broadcast_to(aligned, (NZ,) + aligned.shape))
    scales = call(
        functools.partial(scale_body, model_width=model_width),
        jax.ShapeDtypeStruct((NS, NS, LANES), F32),
        [SMEM, VMEM, VMEM],
        (place, parts, squares),
    )
    scales = lax.all_to_all(scales, "section", 0, 0)

    by_micro = (MICRO, tokens // MICRO, width)
    at_rows = pl.BlockSpec((MICRO, LANES, width), lambda i: (0, i, 0))
    at_half = pl.BlockSpec((LANES, width), lambda i: (i, 0))
    input_grads = pl.pallas_call(
        total_body,
        grid=(tokens // MICRO // LANES,),
        out_shape=jax.ShapeDtypeStruct(by_micro, BF16),
        in_specs=[
            SMEM,
            pl.BlockSpec((NS, MICRO, LANES, width), lambda i: (0, 0, i, 0)),
            pl.BlockSpec((NS, NS, LANES), lambda i: (0, 0, 0)),
            at_rows,
            at_rows,
            at_half,
            at_half,
            at_rows,
        ],
        out_specs=at_rows,
        compiler_params=pltpu.CompilerParams(vmem_limit_bytes=28 * 2**20),
    )(
        place,
        raw_all,
        scales,
        direct.reshape(by_micro),
        other.reshape(by_micro),
        above,
        above_other,
        top_grad,
    )
    return (input_grads[None], weight_grads)


def solution(mesh):
    in_specs = (
        P("section", None),
        P("section", None, "dp", "tensor"),
        P("section", "tensor"),
        P("section", "tensor", None),
        P("section", None, ("dp", "tensor"), None),
        P(None, "dp", "tensor"),
    )
    out_specs = (P("section", None, "dp", "tensor"), P("section", "tensor", "dp"))
    return jax.shard_map(shards, mesh=mesh, in_specs=in_specs, out_specs=out_specs, check_vma=False)
```

```python
import functools

import jax
import jax.numpy as jnp
from jax import lax
from jax.experimental import pallas as pl
from jax.experimental.pallas import tpu as pltpu
from jax.sharding import PartitionSpec as P

EPSILON = 1e-06
NY, NZ, NX, NS = 4, 4, 4, 8
MICRO, ROWS, LANES = 2, 16, 128
BLOCKS = NY * NZ
SHARE, HALF = MICRO * ROWS, BLOCKS * ROWS
LINES = MICRO * HALF // LANES
F32, BF16 = jnp.float32, jnp.bfloat16
VMEM = pl.BlockSpec(memory_space=pltpu.VMEM)
SMEM = pl.BlockSpec(memory_space=pltpu.SMEM)


def y_groups():
    return [[y * NZ + z for y in range(NY)] for z in range(NZ)]


def z_groups():
    return [[y * NZ + z for z in range(NZ)] for y in range(NY)]


def from_y(value, step):
    perm = [((y + step) % NY * NZ + z, y * NZ + z) for y in range(NY) for z in range(NZ)]
    return lax.ppermute(value, "tensor", perm)


def from_z(value, step):
    perm = [(y * NZ + (z + step) % NZ, y * NZ + z) for y in range(NY) for z in range(NZ)]
    return lax.ppermute(value, "tensor", perm)


def from_other_core(value):
    return lax.ppermute(value, "section", [(s, s ^ 1) for s in range(NS)])


def from_chips_above(value, chips):
    return lax.ppermute(value, "section", [(s, s - 2 * chips) for s in range(2 * chips, NS)])


def y_exchange(spread):
    return lax.all_to_all(spread, "tensor", 0, 0, axis_index_groups=y_groups())


def z_exchange(spread):
    return lax.all_to_all(spread, "tensor", 0, 0, axis_index_groups=z_groups())


def call(body, out_shape, specs, args, scratch=(), cost=None):
    return pl.pallas_call(
        body,
        out_shape=out_shape,
        in_specs=specs,
        out_specs=jax.tree.map(lambda _: VMEM, out_shape),
        scratch_shapes=list(scratch),
        compiler_params=pltpu.CompilerParams(vmem_limit_bytes=14 * 2**20),
        cost_estimate=cost,
    )(*args)


def columns(row, count):
    return jnp.transpose(jnp.broadcast_to(row, (LANES, LANES)))[:, :1] + jnp.zeros((LANES, count), F32)


def parted(value):
    high = value.astype(BF16)
    rest = value - high.astype(F32)
    middle = rest.astype(BF16)
    low = (rest - middle.astype(F32)).astype(BF16)
    unused = jnp.zeros((SHARE - 3 * LINES, LANES), F32)
    stacked = [part.astype(F32) for part in (high, middle, low)]
    return jnp.concatenate(stacked + [unused]).astype(BF16)


def joined(block):
    block = block.astype(F32)
    return block[:LINES] + (block[LINES : 2 * LINES] + block[2 * LINES : 3 * LINES])


def row_sums(terms):
    folded = sum(terms[:, k * LANES : (k + 1) * LANES] for k in range(terms.shape[1] // LANES))
    return jnp.sum(jnp.transpose(folded), axis=0, keepdims=True)


def pack_body(place, kv_ref, stashed, out_ref):
    kvw = kv_ref.shape[1]
    swap = place[2]
    sums = []
    for chunk in range(LINES):
        m, at = chunk * LANES // HALF, chunk * LANES % HALF
        hidden = stashed[m ^ swap, at : at + LANES].astype(F32)
        sums.append(row_sums(hidden * hidden))
    squares = parted(jnp.concatenate(sums))
    for z in range(NZ):
        out_ref[z, :, :kvw] = kv_ref[...]
        out_ref[z, :, kvw:] = squares


def spread_body(place, kv_ref, out_ref):
    kvw = kv_ref.shape[2] - LANES
    squares = parted(sum(joined(kv_ref[z, :, kvw:]) for z in range(NZ)))
    for step in range(1, NZ):
        block = kv_ref[lax.rem(place[0] + step, NZ), :, :kvw]
        rows = slice((step - 1) * SHARE, step * SHARE)
        for y in range(NY):
            out_ref[y, rows, :kvw] = block
            out_ref[y, rows, kvw:] = squares


def back_body(place, own0, own1, own2, own3, others, weight, gains, stashed, direct, direct16, aligned, squares, grad):
    tz, ty, swap = place[0], place[1], place[2]
    kvw = weight.shape[1]
    width = weight.shape[0]
    model_width = width * BLOCKS
    dims = (((1,), (1,)), ((), ()))
    squares[...] = sum(joined(others[y, :SHARE, kvw:]) for y in range(NY))

    def put(product, blocks):
        for at, (y, step) in enumerate(blocks):
            for m in range(MICRO):
                row = (at * MICRO + m) * ROWS
                grad[m, y * NZ + lax.rem(tz + step, NZ)] = product[row : row + ROWS]

    mine = jnp.concatenate([ref[...] for ref in (own0, own1, own2, own3)])
    product = lax.dot_general(mine, weight[...], dims, preferred_element_type=F32)
    put(product, [(lax.rem(ty + k, NY), 0) for k in range(NY)])
    for y in range(NY):
        product = lax.dot_general(others[y, :, :kvw], weight[...], dims, preferred_element_type=F32)
        put(product, [(y, step) for step in range(1, NZ)])
    gain = gains[...].astype(F32)
    per = LANES // ROWS
    for chunk in range(MICRO * BLOCKS // per):
        m, first = chunk * per // BLOCKS, chunk * per % BLOCKS
        gained = grad[m, first : first + per].reshape(LANES, width) * gain
        hidden = stashed[m ^ swap, first * ROWS : (first + per) * ROWS].astype(F32)
        inverse = 1.0 / jnp.sqrt(squares[chunk : chunk + 1] / model_width + EPSILON)
        here = gained * columns(inverse, width)
        direct[chunk * LANES : (chunk + 1) * LANES] = here
        direct16[chunk * LANES : (chunk + 1) * LANES] = here.astype(BF16)
        total = row_sums(gained * hidden)
        for y in range(NY):
            aligned[y, chunk : chunk + 1] = total


def half_body(place, direct, other, out_ref):
    rows = out_ref.shape[0]
    at = pl.ds(pl.multiple_of(place[3] * rows, rows), rows)
    out_ref[...] = (direct[at] + other[at].astype(F32)).astype(BF16)


def outer_body(place, own0, own1, own2, own3, others, gains, stashed, squares, out_ref, normed, left):
    tz, ty, swap = place[0], place[1], place[2]
    width = out_ref.shape[1]
    model_width = width * BLOCKS
    gain = gains[...].astype(F32)
    per = LANES // ROWS
    for chunk in range(MICRO * BLOCKS // per):
        m, first = chunk * per // BLOCKS, chunk * per % BLOCKS
        hidden = stashed[m ^ swap, first * ROWS : (first + per) * ROWS].astype(F32)
        inverse = 1.0 / jnp.sqrt(squares[chunk : chunk + 1] / model_width + EPSILON)
        here = gain * hidden * columns(inverse, width)
        normed[m, first : first + per] = here.astype(BF16).reshape(per, ROWS, width)
    blocks = [(lax.rem(ty + k, NY), 0) for k in range(NY)]
    blocks += [(y, step) for y in range(NY) for step in range(1, NZ)]
    for at, (y, step) in enumerate(blocks):
        for m in range(MICRO):
            row = (at * MICRO + m) * ROWS
            left[row : row + ROWS] = normed[m, y * NZ + lax.rem(tz + step, NZ)]
    turned = jnp.transpose(left[...])
    for x in range(NX):
        at = slice(x * width, (x + 1) * width)
        mine = [ref[:, at] for ref in (own0, own1, own2, own3)]
        right = jnp.concatenate(mine + [others[y, :, at] for y in range(NY)])
        out_ref[x] = jnp.dot(turned, right, preferred_element_type=F32).astype(out_ref.dtype)


def scale_body(place, parts, squares, out_ref, *, model_width):
    mean = squares[...] / model_width + EPSILON
    total = parts[0] + parts[1] + parts[2] + parts[3]
    scale = total / (model_width * (mean * jnp.sqrt(mean)))
    swap = jnp.full((NS - LINES, LANES), place[2], jnp.int32).astype(F32)
    value = jnp.concatenate([scale, swap])
    for section in range(NS):
        out_ref[section] = value


def total_body(place, raw, scales, direct, other, above1, above2, above3, above_other, top, out_ref):
    section, core = place[4], place[3]
    rows, width = raw.shape[2], raw.shape[3]
    chunk = pl.program_id(0)
    use_other = jnp.where(core == 0, 1.0, 0.0)
    fixes = [jnp.zeros((rows, width), F32) for _ in range(MICRO)]
    turned = []
    for m in range(MICRO):
        row = m * (BLOCKS * ROWS // LANES) + chunk
        turned.append(jnp.transpose(scales[:, pl.ds(row, 1)].reshape(NS, LANES)))
    for u in range(NS):
        live = jnp.where(u >= section, 1.0, 0.0)
        swapped = scales[u, NS - 1 : NS, :1] != 0.0
        slots = [raw[u, k].astype(F32) for k in range(MICRO)]
        for m in range(MICRO):
            hidden = jnp.where(swapped, slots[1 - m], slots[m])
            fixes[m] = fixes[m] + hidden * (turned[m][:, u : u + 1] * live)
    above = above1[...].astype(F32) + above2[...].astype(F32) + above3[...].astype(F32)
    for m in range(MICRO):
        mine = jnp.where(core == m, above, above_other[...].astype(F32))
        value = top[m].astype(F32) + direct[m] + use_other * other[m].astype(F32) + mine - fixes[m]
        out_ref[m] = value.astype(BF16)


def shards(plan, stashed, norm_gain, kv_weight, kv_grad, top_grad):
    section = lax.axis_index("section")
    core = section % 2
    index = lax.axis_index("tensor")
    tz, ty = index % NZ, index // NZ
    width = stashed.shape[-1]
    tokens = MICRO * BLOCKS * ROWS
    model_width = width * BLOCKS
    lines = tokens // LANES
    place = jnp.stack([tz, ty, plan[0, 0], core, section]).astype(jnp.int32)
    slots, weight = stashed[0], kv_weight[0]
    kvw = weight.shape[-1]
    kv0 = kv_grad.reshape(SHARE, kvw)
    half = (tokens // 2, width)

    shape = jax.ShapeDtypeStruct((NZ, SHARE, kvw + LANES), BF16)
    packed = call(pack_body, shape, [SMEM, VMEM, VMEM], (place, kv0, slots))
    packed, kv_y = lax.optimization_barrier((packed, kv0))
    kv_z = z_exchange(packed)
    own = [kv_y] + [from_y(kv_y, d) for d in (1, 2, 3)]
    kv_z, own, slots_later = lax.optimization_barrier((kv_z, own, slots))

    raw_all = lax.all_gather(slots_later, "section")
    shape = jax.ShapeDtypeStruct((NY, (NZ - 1) * SHARE, kvw + LANES), BF16)
    others = y_exchange(call(spread_body, shape, [SMEM, VMEM], (place, kv_z)))

    flops = 2 * tokens * width * kvw
    direct, direct16, aligned, squares = call(
        back_body,
        (
            jax.ShapeDtypeStruct((tokens, width), F32),
            jax.ShapeDtypeStruct((tokens, width), BF16),
            jax.ShapeDtypeStruct((NY, lines, LANES), F32),
            jax.ShapeDtypeStruct((lines, LANES), F32),
        ),
        [SMEM] + [VMEM] * 8,
        (place, *own, others, weight, norm_gain, slots),
        [pltpu.VMEM((MICRO, BLOCKS, ROWS, width), F32)],
        pl.CostEstimate(flops=flops, bytes_accessed=6 * 2**20, transcendentals=0),
    )
    other = from_other_core(direct16)
    aligned = y_exchange(aligned)
    other, aligned = lax.optimization_barrier((other, aligned))
    aligned = jnp.sum(aligned, axis=0)

    chip = call(half_body, jax.ShapeDtypeStruct(half, BF16), [SMEM, VMEM, VMEM], (place, direct, other))
    above = [from_chips_above(chip, d) for d in (1, 2, 3)]
    above_other = from_other_core(sum(part.astype(F32) for part in above).astype(BF16))

    own, others, _ = lax.optimization_barrier((own, others, above[0]))
    local = call(
        outer_body,
        jax.ShapeDtypeStruct((NX, width, width), BF16),
        [SMEM] + [VMEM] * 8,
        (place, *own, others, norm_gain, slots, squares),
        [pltpu.VMEM((MICRO, BLOCKS, ROWS, width), BF16), pltpu.VMEM((tokens, width), BF16)],
        pl.CostEstimate(flops=flops, bytes_accessed=6 * 2**20, transcendentals=0),
    )
    summed = lax.psum_scatter(local, "dp", scatter_dimension=0)
    weight_grads = (summed.astype(F32) / (MICRO * NX)).astype(BF16)[None]

    parts = z_exchange(jnp.broadcast_to(aligned, (NZ,) + aligned.shape))
    parts, raw_all = lax.optimization_barrier((parts, raw_all))
    scales = call(
        functools.partial(scale_body, model_width=model_width),
        jax.ShapeDtypeStruct((NS, NS, LANES), F32),
        [SMEM, VMEM, VMEM],
        (place, parts, squares),
    )
    scales = lax.all_to_all(scales, "section", 0, 0)

    by_micro = (MICRO, tokens // MICRO, width)
    at_rows = pl.BlockSpec((MICRO, LANES, width), lambda i: (0, i, 0))
    at_half = pl.BlockSpec((LANES, width), lambda i: (i, 0))
    input_grads = pl.pallas_call(
        total_body,
        grid=(tokens // MICRO // LANES,),
        out_shape=jax.ShapeDtypeStruct(by_micro, BF16),
        in_specs=[
            SMEM,
            pl.BlockSpec((NS, MICRO, LANES, width), lambda i: (0, 0, i, 0)),
            pl.BlockSpec((NS, NS, LANES), lambda i: (0, 0, 0)),
            at_rows,
            at_rows,
            at_half,
            at_half,
            at_half,
            at_half,
            at_rows,
        ],
        out_specs=at_rows,
        compiler_params=pltpu.CompilerParams(vmem_limit_bytes=14 * 2**20),
    )(
        place,
        raw_all,
        scales,
        direct.reshape(by_micro),
        other.reshape(by_micro),
        *above,
        above_other,
        top_grad,
    )
    return (input_grads[None], weight_grads)


def solution(mesh):
    in_specs = (
        P("section", None),
        P("section", None, "dp", "tensor"),
        P("section", "tensor"),
        P("section", "tensor", None),
        P("section", None, ("dp", "tensor"), None),
        P(None, "dp", "tensor"),
    )
    out_specs = (P("section", None, "dp", "tensor"), P("section", "tensor", "dp"))
    return jax.shard_map(shards, mesh=mesh, in_specs=in_specs, out_specs=out_specs, check_vma=False)
```

```python
import functools

import jax
import jax.numpy as jnp
from jax import lax
from jax.experimental import pallas as pl
from jax.experimental.pallas import tpu as pltpu
from jax.sharding import PartitionSpec as P

EPSILON = 1e-06
NY, NZ, NX, NS = 4, 4, 4, 8
MICRO, ROWS, LANES = 2, 16, 128
BLOCKS = NY * NZ
SHARE, HALF = MICRO * ROWS, BLOCKS * ROWS
LINES = MICRO * HALF // LANES
F32, BF16 = jnp.float32, jnp.bfloat16
VMEM = pl.BlockSpec(memory_space=pltpu.VMEM)
SMEM = pl.BlockSpec(memory_space=pltpu.SMEM)


def y_groups():
    return [[y * NZ + z for y in range(NY)] for z in range(NZ)]


def z_groups():
    return [[y * NZ + z for z in range(NZ)] for y in range(NY)]


def from_y(value, step):
    perm = [((y + step) % NY * NZ + z, y * NZ + z) for y in range(NY) for z in range(NZ)]
    return lax.ppermute(value, "tensor", perm)


def from_z(value, step):
    perm = [(y * NZ + (z + step) % NZ, y * NZ + z) for y in range(NY) for z in range(NZ)]
    return lax.ppermute(value, "tensor", perm)


def from_other_core(value):
    return lax.ppermute(value, "section", [(s, s ^ 1) for s in range(NS)])


def from_chips_above(value, chips):
    return lax.ppermute(value, "section", [(s, s - 2 * chips) for s in range(2 * chips, NS)])


def y_exchange(spread):
    return lax.all_to_all(spread, "tensor", 0, 0, axis_index_groups=y_groups())


def z_exchange(spread):
    return lax.all_to_all(spread, "tensor", 0, 0, axis_index_groups=z_groups())


def call(body, out_shape, specs, args, scratch=(), cost=None, limit=14):
    return pl.pallas_call(
        body,
        out_shape=out_shape,
        in_specs=specs,
        out_specs=jax.tree.map(lambda _: VMEM, out_shape),
        scratch_shapes=list(scratch),
        compiler_params=pltpu.CompilerParams(vmem_limit_bytes=limit * 2**20),
        cost_estimate=cost,
    )(*args)


def columns(row, count):
    return jnp.transpose(jnp.broadcast_to(row, (LANES, LANES)))[:, :1] + jnp.zeros((LANES, count), F32)


def parted(value):
    high = value.astype(BF16)
    rest = value - high.astype(F32)
    middle = rest.astype(BF16)
    low = (rest - middle.astype(F32)).astype(BF16)
    unused = jnp.zeros((SHARE - 3 * LINES, LANES), F32)
    stacked = [part.astype(F32) for part in (high, middle, low)]
    return jnp.concatenate(stacked + [unused]).astype(BF16)


def joined(block):
    block = block.astype(F32)
    return block[:LINES] + (block[LINES : 2 * LINES] + block[2 * LINES : 3 * LINES])


def row_sums(terms):
    folded = sum(terms[:, k * LANES : (k + 1) * LANES] for k in range(terms.shape[1] // LANES))
    return jnp.sum(jnp.transpose(folded), axis=0, keepdims=True)


def pack_body(plan, kv_ref, stashed, out_ref):
    kvw = kv_ref.shape[1]
    swap = plan[0, 0]
    sums = []
    for chunk in range(LINES):
        m, at = chunk * LANES // HALF, chunk * LANES % HALF
        hidden = stashed[m ^ swap, at : at + LANES].astype(F32)
        sums.append(row_sums(hidden * hidden))
    squares = parted(jnp.concatenate(sums))
    for z in range(NZ):
        out_ref[z, :, :kvw] = kv_ref[...]
        out_ref[z, :, kvw:] = squares


def spread_body(place, kv_ref, out_ref):
    kvw = kv_ref.shape[2] - LANES
    squares = parted(sum(joined(kv_ref[z, :, kvw:]) for z in range(NZ)))
    for step in range(1, NZ):
        block = kv_ref[lax.rem(place[0] + step, NZ), :, :kvw]
        rows = slice((step - 1) * SHARE, step * SHARE)
        for y in range(NY):
            out_ref[y, rows, :kvw] = block
            out_ref[y, rows, kvw:] = squares


def back_body(place, own0, own1, own2, own3, others, weight, gains, saved, direct, direct16, aligned, squares, grad):
    tz, ty = place[0], place[1]
    kvw = weight.shape[1]
    width = weight.shape[0]
    model_width = width * BLOCKS
    dims = (((1,), (1,)), ((), ()))
    squares[...] = sum(joined(others[y, :SHARE, kvw:]) for y in range(NY))

    def put(product, blocks):
        for at, (y, step) in enumerate(blocks):
            for m in range(MICRO):
                row = (at * MICRO + m) * ROWS
                grad[m, y * NZ + lax.rem(tz + step, NZ)] = product[row : row + ROWS]

    mine = jnp.concatenate([ref[...] for ref in (own0, own1, own2, own3)])
    product = lax.dot_general(mine, weight[...], dims, preferred_element_type=F32)
    put(product, [(lax.rem(ty + k, NY), 0) for k in range(NY)])
    for y in range(NY):
        product = lax.dot_general(others[y, :, :kvw], weight[...], dims, preferred_element_type=F32)
        put(product, [(y, step) for step in range(1, NZ)])
    gain = gains[...].astype(F32)
    per = LANES // ROWS
    for chunk in range(MICRO * BLOCKS // per):
        m, first = chunk * per // BLOCKS, chunk * per % BLOCKS
        gained = grad[m, first : first + per].reshape(LANES, width) * gain
        hidden = saved[m, first * ROWS : (first + per) * ROWS].astype(F32)
        inverse = 1.0 / jnp.sqrt(squares[chunk : chunk + 1] / model_width + EPSILON)
        here = gained * columns(inverse, width)
        direct[chunk * LANES : (chunk + 1) * LANES] = here
        direct16[chunk * LANES : (chunk + 1) * LANES] = here.astype(BF16)
        total = row_sums(gained * hidden)
        for y in range(NY):
            aligned[y, chunk : chunk + 1] = total


def half_body(place, direct, other, out_ref):
    rows = out_ref.shape[0]
    at = pl.ds(pl.multiple_of(place[2] * rows, rows), rows)
    out_ref[...] = (direct[at] + other[at].astype(F32)).astype(BF16)


def outer_body(place, own0, own1, own2, own3, others, gains, saved, squares, out_ref, normed, left):
    tz, ty = place[0], place[1]
    width = out_ref.shape[1]
    model_width = width * BLOCKS
    gain = gains[...].astype(F32)
    per = LANES // ROWS
    for chunk in range(MICRO * BLOCKS // per):
        m, first = chunk * per // BLOCKS, chunk * per % BLOCKS
        hidden = saved[m, first * ROWS : (first + per) * ROWS].astype(F32)
        inverse = 1.0 / jnp.sqrt(squares[chunk : chunk + 1] / model_width + EPSILON)
        here = gain * hidden * columns(inverse, width)
        normed[m, first : first + per] = here.astype(BF16).reshape(per, ROWS, width)
    blocks = [(lax.rem(ty + k, NY), 0) for k in range(NY)]
    blocks += [(y, step) for y in range(NY) for step in range(1, NZ)]
    for at, (y, step) in enumerate(blocks):
        for m in range(MICRO):
            row = (at * MICRO + m) * ROWS
            left[row : row + ROWS] = normed[m, y * NZ + lax.rem(tz + step, NZ)]
    turned = jnp.transpose(left[...])
    for x in range(NX):
        at = slice(x * width, (x + 1) * width)
        mine = [ref[:, at] for ref in (own0, own1, own2, own3)]
        right = jnp.concatenate(mine + [others[y, :, at] for y in range(NY)])
        product = jnp.dot(turned, right, preferred_element_type=F32)
        out_ref[x] = (product / (MICRO * NX)).astype(BF16)


def scale_body(parts, squares, out_ref, *, model_width):
    mean = squares[...] / model_width + EPSILON
    total = parts[0] + parts[1] + parts[2] + parts[3]
    scale = total / (model_width * (mean * jnp.sqrt(mean)))
    for section in range(NS):
        out_ref[section] = scale


def total_body(place, saved, scales, direct, other, above1, above2, above3, above_other, top, out_ref, held, sems):
    copies = [pltpu.make_async_copy(saved.at[u], held.at[u], sems.at[u]) for u in range(NS)]
    for copy in copies:
        copy.start()
    section, core = place[3], place[2]
    use_other = jnp.where(core == 0, 1.0, 0.0)
    live = lax.broadcasted_iota(jnp.int32, (LANES, NS), 1) >= section
    for copy in copies:
        copy.wait()
    step = 2 * ROWS
    for m in range(MICRO):
        for first in range(0, HALF, LANES):
            scale = scales[:, (m * HALF + first) // LANES].reshape(NS, LANES)
            scale = jnp.where(live, jnp.transpose(scale), 0.0)
            for row in range(0, LANES, step):
                at = slice(first + row, first + row + step)
                above = above1[at].astype(F32) + above2[at].astype(F32) + above3[at].astype(F32)
                above = jnp.where(core == m, above, above_other[at].astype(F32))
                value = top[m, at].astype(F32) + direct[m, at] + above
                value = value + use_other * other[m, at].astype(F32)
                for u in range(NS):
                    value = value - held[u, m, at].astype(F32) * scale[row : row + step, u : u + 1]
                out_ref[m, at] = value.astype(BF16)


def shards(plan, stashed, norm_gain, kv_weight, kv_grad, top_grad):
    section = lax.axis_index("section")
    core = section % 2
    index = lax.axis_index("tensor")
    tz, ty = index % NZ, index // NZ
    width = stashed.shape[-1]
    tokens = MICRO * BLOCKS * ROWS
    model_width = width * BLOCKS
    lines = tokens // LANES
    place = jnp.stack([tz, ty, core, section]).astype(jnp.int32)
    slots, weight = stashed[0], kv_weight[0]
    kvw = weight.shape[-1]
    kv0 = kv_grad.reshape(SHARE, kvw)
    half = (tokens // 2, width)

    shape = jax.ShapeDtypeStruct((NZ, SHARE, kvw + LANES), BF16)
    packed = call(pack_body, shape, [SMEM, VMEM, VMEM], (plan, kv0, slots))
    packed, kv_y, slots = lax.optimization_barrier((packed, kv0, slots))
    kv_z = z_exchange(packed)
    own = [kv_y] + [from_y(kv_y, d) for d in (1, 2, 3)]
    hidden = jnp.where(plan[0, 0] == 0, slots, slots[::-1])
    kv_z, own, hidden = lax.optimization_barrier((kv_z, own, hidden))

    hidden_all = lax.all_gather(hidden, "section")
    shape = jax.ShapeDtypeStruct((NY, (NZ - 1) * SHARE, kvw + LANES), BF16)
    others = y_exchange(call(spread_body, shape, [SMEM, VMEM], (place, kv_z)))

    flops = 2 * tokens * width * kvw
    direct, direct16, aligned, squares = call(
        back_body,
        (
            jax.ShapeDtypeStruct((tokens, width), F32),
            jax.ShapeDtypeStruct((tokens, width), BF16),
            jax.ShapeDtypeStruct((NY, lines, LANES), F32),
            jax.ShapeDtypeStruct((lines, LANES), F32),
        ),
        [SMEM] + [VMEM] * 8,
        (place, *own, others, weight, norm_gain, hidden),
        [pltpu.VMEM((MICRO, BLOCKS, ROWS, width), F32)],
        pl.CostEstimate(flops=flops, bytes_accessed=6 * 2**20, transcendentals=0),
    )
    other = from_other_core(direct16)
    aligned = y_exchange(aligned)
    other, aligned = lax.optimization_barrier((other, aligned))
    aligned = jnp.sum(aligned, axis=0)

    chip = call(half_body, jax.ShapeDtypeStruct(half, BF16), [SMEM, VMEM, VMEM], (place, direct, other))
    above = [from_chips_above(chip, d) for d in (1, 2, 3)]
    parts = z_exchange(jnp.broadcast_to(aligned, (NZ,) + aligned.shape))
    above, parts, hidden_all = lax.optimization_barrier((above, parts, hidden_all))
    above_other = from_other_core(sum(part.astype(F32) for part in above).astype(BF16))

    own, others, _ = lax.optimization_barrier((own, others, other))
    local = call(
        outer_body,
        jax.ShapeDtypeStruct((NX, width, width), BF16),
        [SMEM] + [VMEM] * 8,
        (place, *own, others, norm_gain, hidden, squares),
        [pltpu.VMEM((MICRO, BLOCKS, ROWS, width), BF16), pltpu.VMEM((tokens, width), BF16)],
        pl.CostEstimate(flops=flops, bytes_accessed=6 * 2**20, transcendentals=0),
    )
    weight_grads = lax.psum_scatter(local, "dp", scatter_dimension=0)[None]

    scales = call(
        functools.partial(scale_body, model_width=model_width),
        jax.ShapeDtypeStruct((NS, lines, LANES), F32),
        [VMEM, VMEM],
        (parts, squares),
    )
    scales = lax.all_to_all(scales, "section", 0, 0)
    by_micro = (MICRO, tokens // MICRO, width)
    input_grads = call(
        total_body,
        jax.ShapeDtypeStruct(by_micro, BF16),
        [SMEM, pl.BlockSpec(memory_space=pltpu.HBM)] + [VMEM] * 8,
        (
            place,
            hidden_all,
            scales,
            direct.reshape(by_micro),
            other.reshape(by_micro),
            *above,
            above_other,
            top_grad,
        ),
        [pltpu.VMEM((NS,) + by_micro, BF16), pltpu.SemaphoreType.DMA((NS,))],
        limit=48,
    )
    return (input_grads[None], weight_grads)


def solution(mesh):
    in_specs = (
        P("section", None),
        P("section", None, "dp", "tensor"),
        P("section", "tensor"),
        P("section", "tensor", None),
        P("section", None, ("dp", "tensor"), None),
        P(None, "dp", "tensor"),
    )
    out_specs = (P("section", None, "dp", "tensor"), P("section", "tensor", "dp"))
    return jax.shard_map(shards, mesh=mesh, in_specs=in_specs, out_specs=out_specs, check_vma=False)
```

```python
import functools

import jax
import jax.numpy as jnp
from jax import lax
from jax.experimental import pallas as pl
from jax.experimental.pallas import tpu as pltpu
from jax.sharding import PartitionSpec as P

EPSILON = 1e-06
NY, NZ, NX, NS = 4, 4, 4, 8
MICRO, ROWS, LANES = 2, 16, 128
BLOCKS = NY * NZ
SHARE, HALF = MICRO * ROWS, BLOCKS * ROWS
LINES = MICRO * HALF // LANES
F32, BF16 = jnp.float32, jnp.bfloat16
VMEM = pl.BlockSpec(memory_space=pltpu.VMEM)
SMEM = pl.BlockSpec(memory_space=pltpu.SMEM)


def y_groups():
    return [[y * NZ + z for y in range(NY)] for z in range(NZ)]


def z_groups():
    return [[y * NZ + z for z in range(NZ)] for y in range(NY)]


def from_y(value, step):
    perm = [((y + step) % NY * NZ + z, y * NZ + z) for y in range(NY) for z in range(NZ)]
    return lax.ppermute(value, "tensor", perm)


def from_z(value, step):
    perm = [(y * NZ + (z + step) % NZ, y * NZ + z) for y in range(NY) for z in range(NZ)]
    return lax.ppermute(value, "tensor", perm)


def from_other_core(value):
    return lax.ppermute(value, "section", [(s, s ^ 1) for s in range(NS)])


def from_chips_above(value, chips):
    return lax.ppermute(value, "section", [(s, s - 2 * chips) for s in range(2 * chips, NS)])


def y_exchange(spread):
    return lax.all_to_all(spread, "tensor", 0, 0, axis_index_groups=y_groups())


def z_exchange(spread):
    return lax.all_to_all(spread, "tensor", 0, 0, axis_index_groups=z_groups())


def call(body, out_shape, specs, args, scratch=(), cost=None, limit=14):
    return pl.pallas_call(
        body,
        out_shape=out_shape,
        in_specs=specs,
        out_specs=jax.tree.map(lambda _: VMEM, out_shape),
        scratch_shapes=list(scratch),
        compiler_params=pltpu.CompilerParams(vmem_limit_bytes=limit * 2**20),
        cost_estimate=cost,
    )(*args)


def columns(row, count):
    return jnp.transpose(jnp.broadcast_to(row, (LANES, LANES)))[:, :1] + jnp.zeros((LANES, count), F32)


def parted(value):
    high = value.astype(BF16)
    rest = value - high.astype(F32)
    middle = rest.astype(BF16)
    low = (rest - middle.astype(F32)).astype(BF16)
    unused = jnp.zeros((SHARE - 3 * LINES, LANES), F32)
    stacked = [part.astype(F32) for part in (high, middle, low)]
    return jnp.concatenate(stacked + [unused]).astype(BF16)


def joined(block):
    block = block.astype(F32)
    return block[:LINES] + (block[LINES : 2 * LINES] + block[2 * LINES : 3 * LINES])


def row_sums(terms):
    folded = sum(terms[:, k * LANES : (k + 1) * LANES] for k in range(terms.shape[1] // LANES))
    return jnp.sum(jnp.transpose(folded), axis=0, keepdims=True)


def pack_body(plan, kv_ref, stashed, out_ref):
    kvw = kv_ref.shape[1]
    swap = plan[0, 0]
    sums = []
    for chunk in range(LINES):
        m, at = chunk * LANES // HALF, chunk * LANES % HALF
        hidden = stashed[m ^ swap, at : at + LANES].astype(F32)
        sums.append(row_sums(hidden * hidden))
    squares = parted(jnp.concatenate(sums))
    for z in range(NZ):
        out_ref[z, :, :kvw] = kv_ref[...]
        out_ref[z, :, kvw:] = squares


def spread_body(place, kv_ref, out_ref):
    kvw = kv_ref.shape[2] - LANES
    squares = parted(sum(joined(kv_ref[z, :, kvw:]) for z in range(NZ)))
    for step in range(1, NZ):
        block = kv_ref[lax.rem(place[0] + step, NZ), :, :kvw]
        rows = slice((step - 1) * SHARE, step * SHARE)
        for y in range(NY):
            out_ref[y, rows, :kvw] = block
            out_ref[y, rows, kvw:] = squares


def back_body(place, own0, own1, own2, own3, others, weight, gains, saved, direct, direct16, aligned, squares, grad):
    tz, ty = place[0], place[1]
    kvw = weight.shape[1]
    width = weight.shape[0]
    model_width = width * BLOCKS
    dims = (((1,), (1,)), ((), ()))
    squares[...] = sum(joined(others[y, :SHARE, kvw:]) for y in range(NY))

    def put(product, blocks):
        for at, (y, step) in enumerate(blocks):
            for m in range(MICRO):
                row = (at * MICRO + m) * ROWS
                grad[m, y * NZ + lax.rem(tz + step, NZ)] = product[row : row + ROWS]

    mine = jnp.concatenate([ref[...] for ref in (own0, own1, own2, own3)])
    product = lax.dot_general(mine, weight[...], dims, preferred_element_type=F32)
    put(product, [(lax.rem(ty + k, NY), 0) for k in range(NY)])
    rest = others[:, :, :kvw].reshape(NY * (NZ - 1) * SHARE, kvw)
    product = lax.dot_general(rest, weight[...], dims, preferred_element_type=F32)
    put(product, [(y, step) for y in range(NY) for step in range(1, NZ)])
    gain = gains[...].astype(F32)
    per = LANES // ROWS
    for chunk in range(MICRO * BLOCKS // per):
        m, first = chunk * per // BLOCKS, chunk * per % BLOCKS
        gained = grad[m, first : first + per].reshape(LANES, width) * gain
        hidden = saved[m, first * ROWS : (first + per) * ROWS].astype(F32)
        inverse = 1.0 / jnp.sqrt(squares[chunk : chunk + 1] / model_width + EPSILON)
        here = gained * columns(inverse, width)
        direct[chunk * LANES : (chunk + 1) * LANES] = here
        direct16[chunk * LANES : (chunk + 1) * LANES] = here.astype(BF16)
        total = row_sums(gained * hidden)
        for y in range(NY):
            aligned[y, chunk : chunk + 1] = total


def half_body(place, direct, other, out_ref):
    rows = out_ref.shape[0]
    at = pl.ds(pl.multiple_of(place[2] * rows, rows), rows)
    out_ref[...] = (direct[at] + other[at].astype(F32)).astype(BF16)


def outer_body(place, own0, own1, own2, own3, others, gains, saved, squares, out_ref, normed, left):
    tz, ty = place[0], place[1]
    width = out_ref.shape[1]
    model_width = width * BLOCKS
    gain = gains[...].astype(F32)
    per = LANES // ROWS
    for chunk in range(MICRO * BLOCKS // per):
        m, first = chunk * per // BLOCKS, chunk * per % BLOCKS
        hidden = saved[m, first * ROWS : (first + per) * ROWS].astype(F32)
        inverse = 1.0 / jnp.sqrt(squares[chunk : chunk + 1] / model_width + EPSILON)
        here = gain * hidden * columns(inverse, width)
        normed[m, first : first + per] = here.astype(BF16).reshape(per, ROWS, width)
    blocks = [(lax.rem(ty + k, NY), 0) for k in range(NY)]
    blocks += [(y, step) for y in range(NY) for step in range(1, NZ)]
    for at, (y, step) in enumerate(blocks):
        for m in range(MICRO):
            row = (at * MICRO + m) * ROWS
            left[row : row + ROWS] = normed[m, y * NZ + lax.rem(tz + step, NZ)]
    turned = jnp.transpose(left[...])
    for x in range(NX):
        at = slice(x * width, (x + 1) * width)
        mine = [ref[:, at] for ref in (own0, own1, own2, own3)]
        right = jnp.concatenate(mine + [others[y, :, at] for y in range(NY)])
        product = jnp.dot(turned, right, preferred_element_type=F32)
        out_ref[x] = (product / (MICRO * NX)).astype(BF16)


def scale_body(parts, squares, out_ref, *, model_width):
    mean = squares[...] / model_width + EPSILON
    total = parts[0] + parts[1] + parts[2] + parts[3]
    scale = total / (model_width * (mean * jnp.sqrt(mean)))
    for section in range(NS):
        out_ref[section] = scale


def total_body(place, mine, sibling, scales, direct, other, above1, above2, above3, above_other, top, out_ref):
    chips = NS // 2
    section, core = place[3], place[2]
    use_other = jnp.where(core == 0, 1.0, 0.0)
    order = [2 * c + core for c in range(chips)] + [2 * c + 1 - core for c in range(chips)]
    live = [jnp.where(u >= section, 1.0, 0.0) for u in order]
    step = 2 * ROWS
    for m in range(MICRO):
        for first in range(0, HALF, LANES):
            line = (m * HALF + first) // LANES
            scale = [scales[u, line : line + 1] * on for u, on in zip(order, live)]
            scale = jnp.transpose(jnp.concatenate(scale))
            for row in range(0, LANES, step):
                at = slice(first + row, first + row + step)
                above = above1[at].astype(F32) + above2[at].astype(F32) + above3[at].astype(F32)
                above = jnp.where(core == m, above, above_other[at].astype(F32))
                value = top[m, at].astype(F32) + direct[m, at] + above
                value = value + use_other * other[m, at].astype(F32)
                for k in range(NS):
                    held = mine if k < chips else sibling
                    here = held[k % chips, m, at].astype(F32)
                    value = value - here * scale[row : row + step, k : k + 1]
                out_ref[m, at] = value.astype(BF16)


def shards(plan, stashed, norm_gain, kv_weight, kv_grad, top_grad):
    section = lax.axis_index("section")
    core = section % 2
    index = lax.axis_index("tensor")
    tz, ty = index % NZ, index // NZ
    width = stashed.shape[-1]
    tokens = MICRO * BLOCKS * ROWS
    model_width = width * BLOCKS
    lines = tokens // LANES
    place = jnp.stack([tz, ty, core, section]).astype(jnp.int32)
    slots, weight = stashed[0], kv_weight[0]
    kvw = weight.shape[-1]
    kv0 = kv_grad.reshape(SHARE, kvw)
    half = (tokens // 2, width)

    shape = jax.ShapeDtypeStruct((NZ, SHARE, kvw + LANES), BF16)
    packed = call(pack_body, shape, [SMEM, VMEM, VMEM], (plan, kv0, slots), limit=56)
    packed, kv_y, slots = lax.optimization_barrier((packed, kv0, slots))
    kv_z = z_exchange(packed)
    own = [kv_y] + [from_y(kv_y, d) for d in (1, 2, 3)]
    hidden = jnp.where(plan[0, 0] == 0, slots, slots[::-1])
    kv_z, own, hidden = lax.optimization_barrier((kv_z, own, hidden))

    groups = [list(range(core, NS, 2)) for core in range(2)]
    hidden_all = lax.all_gather(hidden, "section", axis_index_groups=groups)
    shape = jax.ShapeDtypeStruct((NY, (NZ - 1) * SHARE, kvw + LANES), BF16)
    others = y_exchange(call(spread_body, shape, [SMEM, VMEM], (place, kv_z)))

    flops = 2 * tokens * width * kvw
    direct, direct16, aligned, squares = call(
        back_body,
        (
            jax.ShapeDtypeStruct((tokens, width), F32),
            jax.ShapeDtypeStruct((tokens, width), BF16),
            jax.ShapeDtypeStruct((NY, lines, LANES), F32),
            jax.ShapeDtypeStruct((lines, LANES), F32),
        ),
        [SMEM] + [VMEM] * 8,
        (place, *own, others, weight, norm_gain, hidden),
        [pltpu.VMEM((MICRO, BLOCKS, ROWS, width), F32)],
        pl.CostEstimate(flops=flops, bytes_accessed=6 * 2**20, transcendentals=0),
    )
    other = from_other_core(direct16)
    aligned = y_exchange(aligned)
    other, aligned = lax.optimization_barrier((other, aligned))
    aligned = jnp.sum(aligned, axis=0)

    chip = call(half_body, jax.ShapeDtypeStruct(half, BF16), [SMEM, VMEM, VMEM], (place, direct, other))
    above = [from_chips_above(chip, d) for d in (1, 2, 3)]
    parts = z_exchange(jnp.broadcast_to(aligned, (NZ,) + aligned.shape))
    above, parts, hidden_all = lax.optimization_barrier((above, parts, hidden_all))
    sibling_all = from_other_core(hidden_all)
    above_other = from_other_core(sum(part.astype(F32) for part in above).astype(BF16))

    own, others, _ = lax.optimization_barrier((own, others, other))
    local = call(
        outer_body,
        jax.ShapeDtypeStruct((NX, width, width), BF16),
        [SMEM] + [VMEM] * 8,
        (place, *own, others, norm_gain, hidden, squares),
        [pltpu.VMEM((MICRO, BLOCKS, ROWS, width), BF16), pltpu.VMEM((tokens, width), BF16)],
        pl.CostEstimate(flops=flops, bytes_accessed=6 * 2**20, transcendentals=0),
    )
    weight_grads = lax.psum_scatter(local, "dp", scatter_dimension=0)[None]

    scales = call(
        functools.partial(scale_body, model_width=model_width),
        jax.ShapeDtypeStruct((NS, lines, LANES), F32),
        [VMEM, VMEM],
        (parts, squares),
    )
    scales = lax.all_to_all(scales, "section", 0, 0)
    by_micro = (MICRO, tokens // MICRO, width)
    input_grads = call(
        total_body,
        jax.ShapeDtypeStruct(by_micro, BF16),
        [SMEM] + [VMEM] * 10,
        (
            place,
            hidden_all,
            sibling_all,
            scales,
            direct.reshape(by_micro),
            other.reshape(by_micro),
            *above,
            above_other,
            top_grad,
        ),
    )
    return (input_grads[None], weight_grads)


def solution(mesh):
    in_specs = (
        P("section", None),
        P("section", None, "dp", "tensor"),
        P("section", "tensor"),
        P("section", "tensor", None),
        P("section", None, ("dp", "tensor"), None),
        P(None, "dp", "tensor"),
    )
    out_specs = (P("section", None, "dp", "tensor"), P("section", "tensor", "dp"))
    return jax.shard_map(shards, mesh=mesh, in_specs=in_specs, out_specs=out_specs, check_vma=False)
```

```python
import functools

import jax
import jax.numpy as jnp
from jax import lax
from jax.experimental import pallas as pl
from jax.experimental.pallas import tpu as pltpu
from jax.sharding import PartitionSpec as P

EPSILON = 1e-06
NY, NZ, NX, NS = 4, 4, 4, 8
MICRO, ROWS, LANES = 2, 16, 128
BLOCKS = NY * NZ
SHARE, HALF = MICRO * ROWS, BLOCKS * ROWS
LINES = MICRO * HALF // LANES
F32, BF16 = jnp.float32, jnp.bfloat16
VMEM = pl.BlockSpec(memory_space=pltpu.VMEM)
SMEM = pl.BlockSpec(memory_space=pltpu.SMEM)


def y_groups():
    return [[y * NZ + z for y in range(NY)] for z in range(NZ)]


def z_groups():
    return [[y * NZ + z for z in range(NZ)] for y in range(NY)]


def from_y(value, step):
    perm = [((y + step) % NY * NZ + z, y * NZ + z) for y in range(NY) for z in range(NZ)]
    return lax.ppermute(value, "tensor", perm)


def from_z(value, step):
    perm = [(y * NZ + (z + step) % NZ, y * NZ + z) for y in range(NY) for z in range(NZ)]
    return lax.ppermute(value, "tensor", perm)


def from_other_core(value):
    return lax.ppermute(value, "section", [(s, s ^ 1) for s in range(NS)])


def from_chips_above(value, chips):
    return lax.ppermute(value, "section", [(s, s - 2 * chips) for s in range(2 * chips, NS)])


def y_exchange(spread):
    return lax.all_to_all(spread, "tensor", 0, 0, axis_index_groups=y_groups())


def z_exchange(spread):
    return lax.all_to_all(spread, "tensor", 0, 0, axis_index_groups=z_groups())


def call(body, out_shape, specs, args, scratch=(), cost=None, limit=14):
    return pl.pallas_call(
        body,
        out_shape=out_shape,
        in_specs=specs,
        out_specs=jax.tree.map(lambda _: VMEM, out_shape),
        scratch_shapes=list(scratch),
        compiler_params=pltpu.CompilerParams(vmem_limit_bytes=limit * 2**20),
        cost_estimate=cost,
    )(*args)


def columns(row, count):
    return jnp.transpose(jnp.broadcast_to(row, (LANES, LANES)))[:, :1] + jnp.zeros((LANES, count), F32)


def parted(value):
    high = value.astype(BF16)
    rest = value - high.astype(F32)
    middle = rest.astype(BF16)
    low = (rest - middle.astype(F32)).astype(BF16)
    unused = jnp.zeros((SHARE - 3 * LINES, LANES), F32)
    stacked = [part.astype(F32) for part in (high, middle, low)]
    return jnp.concatenate(stacked + [unused]).astype(BF16)


def joined(block):
    block = block.astype(F32)
    return block[:LINES] + (block[LINES : 2 * LINES] + block[2 * LINES : 3 * LINES])


def row_sums(terms):
    folded = sum(terms[:, k * LANES : (k + 1) * LANES] for k in range(terms.shape[1] // LANES))
    return jnp.sum(jnp.transpose(folded), axis=0, keepdims=True)


def pack_body(plan, kv_ref, stashed, out_ref):
    kvw = kv_ref.shape[1]
    swap = plan[0, 0]
    sums = []
    for chunk in range(LINES):
        m, at = chunk * LANES // HALF, chunk * LANES % HALF
        hidden = stashed[m ^ swap, at : at + LANES].astype(F32)
        sums.append(row_sums(hidden * hidden))
    squares = parted(jnp.concatenate(sums))
    for z in range(NZ):
        out_ref[z, :, :kvw] = kv_ref[...]
        out_ref[z, :, kvw:] = squares


def spread_body(place, kv_ref, out_ref):
    kvw = kv_ref.shape[2] - LANES
    squares = parted(sum(joined(kv_ref[z, :, kvw:]) for z in range(NZ)))
    for step in range(1, NZ):
        block = kv_ref[lax.rem(place[0] + step, NZ), :, :kvw]
        rows = slice((step - 1) * SHARE, step * SHARE)
        for y in range(NY):
            out_ref[y, rows, :kvw] = block
            out_ref[y, rows, kvw:] = squares


def back_body(place, own0, own1, own2, own3, others, weight, gains, saved, direct, direct16, aligned, squares, grad):
    tz, ty = place[0], place[1]
    kvw = weight.shape[1]
    width = weight.shape[0]
    model_width = width * BLOCKS
    dims = (((1,), (1,)), ((), ()))
    squares[...] = sum(joined(others[y, :SHARE, kvw:]) for y in range(NY))

    def put(product, blocks):
        for at, (y, step) in enumerate(blocks):
            for m in range(MICRO):
                row = (at * MICRO + m) * ROWS
                grad[m, y * NZ + lax.rem(tz + step, NZ)] = product[row : row + ROWS]

    mine = jnp.concatenate([ref[...] for ref in (own0, own1, own2, own3)])
    product = lax.dot_general(mine, weight[...], dims, preferred_element_type=F32)
    put(product, [(lax.rem(ty + k, NY), 0) for k in range(NY)])
    rest = others[:, :, :kvw].reshape(NY * (NZ - 1) * SHARE, kvw)
    product = lax.dot_general(rest, weight[...], dims, preferred_element_type=F32)
    put(product, [(y, step) for y in range(NY) for step in range(1, NZ)])
    gain = gains[...].astype(F32)
    per = LANES // ROWS
    for chunk in range(MICRO * BLOCKS // per):
        m, first = chunk * per // BLOCKS, chunk * per % BLOCKS
        gained = grad[m, first : first + per].reshape(LANES, width) * gain
        hidden = saved[m, first * ROWS : (first + per) * ROWS].astype(F32)
        inverse = 1.0 / jnp.sqrt(squares[chunk : chunk + 1] / model_width + EPSILON)
        here = gained * columns(inverse, width)
        direct[chunk * LANES : (chunk + 1) * LANES] = here
        direct16[chunk * LANES : (chunk + 1) * LANES] = here.astype(BF16)
        total = row_sums(gained * hidden)
        for y in range(NY):
            aligned[y, chunk : chunk + 1] = total


def half_body(place, direct, other, out_ref):
    rows = out_ref.shape[0]
    at = pl.ds(pl.multiple_of(place[2] * rows, rows), rows)
    out_ref[...] = (direct[at] + other[at].astype(F32)).astype(BF16)


def outer_body(place, own0, own1, own2, own3, others, gains, saved, squares, out_ref, normed, left):
    tz, ty = place[0], place[1]
    width = out_ref.shape[1]
    model_width = width * BLOCKS
    gain = gains[...].astype(F32)
    per = LANES // ROWS
    for chunk in range(MICRO * BLOCKS // per):
        m, first = chunk * per // BLOCKS, chunk * per % BLOCKS
        hidden = saved[m, first * ROWS : (first + per) * ROWS].astype(F32)
        inverse = 1.0 / jnp.sqrt(squares[chunk : chunk + 1] / model_width + EPSILON)
        here = gain * hidden * columns(inverse, width)
        normed[m, first : first + per] = here.astype(BF16).reshape(per, ROWS, width)
    blocks = [(lax.rem(ty + k, NY), 0) for k in range(NY)]
    blocks += [(y, step) for y in range(NY) for step in range(1, NZ)]
    for at, (y, step) in enumerate(blocks):
        for m in range(MICRO):
            row = (at * MICRO + m) * ROWS
            left[row : row + ROWS] = normed[m, y * NZ + lax.rem(tz + step, NZ)]
    turned = jnp.transpose(left[...])
    for x in range(NX):
        at = slice(x * width, (x + 1) * width)
        mine = [ref[:, at] for ref in (own0, own1, own2, own3)]
        right = jnp.concatenate(mine + [others[y, :, at] for y in range(NY)])
        product = jnp.dot(turned, right, preferred_element_type=F32)
        out_ref[x] = (product / (MICRO * NX)).astype(BF16)


def scale_body(parts, squares, out_ref, *, model_width):
    mean = squares[...] / model_width + EPSILON
    total = parts[0] + parts[1] + parts[2] + parts[3]
    scale = total / (model_width * (mean * jnp.sqrt(mean)))
    for section in range(NS):
        out_ref[section] = scale


def fix_body(place, saved, scales, above1, above2, above3, kept, sent):
    section, core = place[3], place[2]
    chips = NS // 2
    chip = section // 2
    chip_at = [jnp.minimum(chip + d, chips - 1) for d in range(chips)]
    step = 2 * ROWS
    for m in range(MICRO):
        for first in range(0, HALF, LANES):
            line = (m * HALF + first) // LANES
            scale = []
            for d in range(chips):
                at = jnp.minimum(section + 2 * d, NS - 1)
                live = jnp.where(chip + d < chips, 1.0, 0.0)
                scale.append(scales[at, line : line + 1] * live)
            scale = jnp.transpose(jnp.concatenate(scale + scale))
            for row in range(0, LANES, step):
                at = slice(first + row, first + row + step)
                here = slice(row, row + step)
                above = above1[at].astype(F32) + above2[at].astype(F32) + above3[at].astype(F32)
                value = jnp.where(core == m, above, 0.0)
                for d in range(1, chips):
                    value = value - saved[chip_at[d], m, at].astype(F32) * scale[here, d : d + 1]
                whole = value - saved[chip, m, at].astype(F32) * scale[here, :1]
                kept[m, at] = whole
                sent[m, at] = jnp.where(core == 1, whole, value).astype(BF16)


def total_body(place, kept, got, direct, other, top, out_ref):
    use_other = jnp.where(place[2] == 0, 1.0, 0.0)
    value = top[...].astype(F32) + direct[...] + use_other * other[...].astype(F32)
    out_ref[...] = (value + (kept[...] + got[...].astype(F32))).astype(BF16)


def shards(plan, stashed, norm_gain, kv_weight, kv_grad, top_grad):
    section = lax.axis_index("section")
    core = section % 2
    index = lax.axis_index("tensor")
    tz, ty = index % NZ, index // NZ
    width = stashed.shape[-1]
    tokens = MICRO * BLOCKS * ROWS
    model_width = width * BLOCKS
    lines = tokens // LANES
    place = jnp.stack([tz, ty, core, section]).astype(jnp.int32)
    slots, weight = stashed[0], kv_weight[0]
    kvw = weight.shape[-1]
    kv0 = kv_grad.reshape(SHARE, kvw)
    half = (tokens // 2, width)

    shape = jax.ShapeDtypeStruct((NZ, SHARE, kvw + LANES), BF16)
    packed = call(pack_body, shape, [SMEM, VMEM, VMEM], (plan, kv0, slots), limit=56)
    packed, kv_y, slots = lax.optimization_barrier((packed, kv0, slots))
    kv_z = z_exchange(packed)
    own = [kv_y] + [from_y(kv_y, d) for d in (1, 2, 3)]
    hidden = jnp.where(plan[0, 0] == 0, slots, slots[::-1])
    kv_z, own, hidden = lax.optimization_barrier((kv_z, own, hidden))

    groups = [list(range(core, NS, 2)) for core in range(2)]
    saved = lax.all_gather(hidden, "section", axis_index_groups=groups)
    shape = jax.ShapeDtypeStruct((NY, (NZ - 1) * SHARE, kvw + LANES), BF16)
    others = y_exchange(call(spread_body, shape, [SMEM, VMEM], (place, kv_z)))

    flops = 2 * tokens * width * kvw
    direct, direct16, aligned, squares = call(
        back_body,
        (
            jax.ShapeDtypeStruct((tokens, width), F32),
            jax.ShapeDtypeStruct((tokens, width), BF16),
            jax.ShapeDtypeStruct((NY, lines, LANES), F32),
            jax.ShapeDtypeStruct((lines, LANES), F32),
        ),
        [SMEM] + [VMEM] * 8,
        (place, *own, others, weight, norm_gain, hidden),
        [pltpu.VMEM((MICRO, BLOCKS, ROWS, width), F32)],
        pl.CostEstimate(flops=flops, bytes_accessed=6 * 2**20, transcendentals=0),
    )
    other = from_other_core(direct16)
    aligned = y_exchange(aligned)
    other, aligned = lax.optimization_barrier((other, aligned))
    aligned = jnp.sum(aligned, axis=0)

    chip = call(half_body, jax.ShapeDtypeStruct(half, BF16), [SMEM, VMEM, VMEM], (place, direct, other))
    above = [from_chips_above(chip, d) for d in (1, 2, 3)]
    parts = z_exchange(jnp.broadcast_to(aligned, (NZ,) + aligned.shape))
    parts, saved = lax.optimization_barrier((parts, saved))

    own, others, _ = lax.optimization_barrier((own, others, other))
    local = call(
        outer_body,
        jax.ShapeDtypeStruct((NX, width, width), BF16),
        [SMEM] + [VMEM] * 8,
        (place, *own, others, norm_gain, hidden, squares),
        [pltpu.VMEM((MICRO, BLOCKS, ROWS, width), BF16), pltpu.VMEM((tokens, width), BF16)],
        pl.CostEstimate(flops=flops, bytes_accessed=6 * 2**20, transcendentals=0),
    )
    weight_grads = lax.psum_scatter(local, "dp", scatter_dimension=0)[None]

    scales = call(
        functools.partial(scale_body, model_width=model_width),
        jax.ShapeDtypeStruct((NS, lines, LANES), F32),
        [VMEM, VMEM],
        (parts, squares),
    )
    scales = lax.all_to_all(scales, "section", 0, 0)
    by_micro = (MICRO, tokens // MICRO, width)
    kept, sent = call(
        fix_body,
        (jax.ShapeDtypeStruct(by_micro, F32), jax.ShapeDtypeStruct(by_micro, BF16)),
        [SMEM] + [VMEM] * 5,
        (place, saved, scales, *above),
    )
    got = from_other_core(sent)
    input_grads = call(
        total_body,
        jax.ShapeDtypeStruct(by_micro, BF16),
        [SMEM] + [VMEM] * 5,
        (place, kept, got, direct.reshape(by_micro), other.reshape(by_micro), top_grad),
    )
    return (input_grads[None], weight_grads)


def solution(mesh):
    in_specs = (
        P("section", None),
        P("section", None, "dp", "tensor"),
        P("section", "tensor"),
        P("section", "tensor", None),
        P("section", None, ("dp", "tensor"), None),
        P(None, "dp", "tensor"),
    )
    out_specs = (P("section", None, "dp", "tensor"), P("section", "tensor", "dp"))
    return jax.shard_map(shards, mesh=mesh, in_specs=in_specs, out_specs=out_specs, check_vma=False)
```

```python
import functools

import jax
import jax.numpy as jnp
from jax import lax
from jax.experimental import pallas as pl
from jax.experimental.pallas import tpu as pltpu
from jax.sharding import PartitionSpec as P

EPSILON = 1e-06
NY, NZ, NX, NS = 4, 4, 4, 8
MICRO, ROWS, LANES = 2, 16, 128
BLOCKS = NY * NZ
SHARE, HALF = MICRO * ROWS, BLOCKS * ROWS
LINES = MICRO * HALF // LANES
F32, BF16 = jnp.float32, jnp.bfloat16
VMEM = pl.BlockSpec(memory_space=pltpu.VMEM)
SMEM = pl.BlockSpec(memory_space=pltpu.SMEM)


def y_groups():
    return [[y * NZ + z for y in range(NY)] for z in range(NZ)]


def z_groups():
    return [[y * NZ + z for z in range(NZ)] for y in range(NY)]


def from_y(value, step):
    perm = [((y + step) % NY * NZ + z, y * NZ + z) for y in range(NY) for z in range(NZ)]
    return lax.ppermute(value, "tensor", perm)


def from_z(value, step):
    perm = [(y * NZ + (z + step) % NZ, y * NZ + z) for y in range(NY) for z in range(NZ)]
    return lax.ppermute(value, "tensor", perm)


def from_other_core(value):
    return lax.ppermute(value, "section", [(s, s ^ 1) for s in range(NS)])


def from_chips_above(value, chips):
    return lax.ppermute(value, "section", [(s, s - 2 * chips) for s in range(2 * chips, NS)])


def y_exchange(spread):
    return lax.all_to_all(spread, "tensor", 0, 0, axis_index_groups=y_groups())


def z_exchange(spread):
    return lax.all_to_all(spread, "tensor", 0, 0, axis_index_groups=z_groups())


def call(body, out_shape, specs, args, scratch=(), cost=None, limit=14):
    return pl.pallas_call(
        body,
        out_shape=out_shape,
        in_specs=specs,
        out_specs=jax.tree.map(lambda _: VMEM, out_shape),
        scratch_shapes=list(scratch),
        compiler_params=pltpu.CompilerParams(vmem_limit_bytes=limit * 2**20),
        cost_estimate=cost,
    )(*args)


def columns(row, count):
    return jnp.transpose(jnp.broadcast_to(row, (LANES, LANES)))[:, :1] + jnp.zeros((LANES, count), F32)


def parted(value):
    high = value.astype(BF16)
    rest = value - high.astype(F32)
    middle = rest.astype(BF16)
    low = (rest - middle.astype(F32)).astype(BF16)
    unused = jnp.zeros((SHARE - 3 * LINES, LANES), F32)
    stacked = [part.astype(F32) for part in (high, middle, low)]
    return jnp.concatenate(stacked + [unused]).astype(BF16)


def joined(block):
    block = block.astype(F32)
    return block[:LINES] + (block[LINES : 2 * LINES] + block[2 * LINES : 3 * LINES])


def row_sums(terms):
    folded = sum(terms[:, k * LANES : (k + 1) * LANES] for k in range(terms.shape[1] // LANES))
    return jnp.sum(jnp.transpose(folded), axis=0, keepdims=True)


def pack_body(plan, kv_ref, stashed, out_ref):
    kvw = kv_ref.shape[1]
    swap = plan[0, 0]
    sums = []
    for chunk in range(LINES):
        m, at = chunk * LANES // HALF, chunk * LANES % HALF
        hidden = stashed[m ^ swap, at : at + LANES].astype(F32)
        sums.append(row_sums(hidden * hidden))
    squares = parted(jnp.concatenate(sums))
    for z in range(NZ):
        out_ref[z, :, :kvw] = kv_ref[...]
        out_ref[z, :, kvw:] = squares


def spread_body(place, kv_ref, out_ref):
    kvw = kv_ref.shape[2] - LANES
    squares = parted(sum(joined(kv_ref[z, :, kvw:]) for z in range(NZ)))
    for step in range(1, NZ):
        block = kv_ref[lax.rem(place[0] + step, NZ), :, :kvw]
        rows = slice((step - 1) * SHARE, step * SHARE)
        for y in range(NY):
            out_ref[y, rows, :kvw] = block
            out_ref[y, rows, kvw:] = squares


def back_body(place, own0, own1, own2, own3, others, weight, gains, saved, direct, direct16, aligned, squares, grad):
    tz, ty = place[0], place[1]
    kvw = weight.shape[1]
    width = weight.shape[0]
    model_width = width * BLOCKS
    dims = (((1,), (1,)), ((), ()))
    squares[...] = sum(joined(others[y, :SHARE, kvw:]) for y in range(NY))

    def put(product, blocks):
        for at, (y, step) in enumerate(blocks):
            for m in range(MICRO):
                row = (at * MICRO + m) * ROWS
                grad[m, y * NZ + lax.rem(tz + step, NZ)] = product[row : row + ROWS]

    mine = jnp.concatenate([ref[...] for ref in (own0, own1, own2, own3)])
    product = lax.dot_general(mine, weight[...], dims, preferred_element_type=F32)
    put(product, [(lax.rem(ty + k, NY), 0) for k in range(NY)])
    rest = others[:, :, :kvw].reshape(NY * (NZ - 1) * SHARE, kvw)
    product = lax.dot_general(rest, weight[...], dims, preferred_element_type=F32)
    put(product, [(y, step) for y in range(NY) for step in range(1, NZ)])
    gain = gains[...].astype(F32)
    per = LANES // ROWS
    for chunk in range(MICRO * BLOCKS // per):
        m, first = chunk * per // BLOCKS, chunk * per % BLOCKS
        gained = grad[m, first : first + per].reshape(LANES, width) * gain
        hidden = saved[m, first * ROWS : (first + per) * ROWS].astype(F32)
        inverse = 1.0 / jnp.sqrt(squares[chunk : chunk + 1] / model_width + EPSILON)
        here = gained * columns(inverse, width)
        direct[chunk * LANES : (chunk + 1) * LANES] = here
        direct16[chunk * LANES : (chunk + 1) * LANES] = here.astype(BF16)
        total = row_sums(gained * hidden)
        for y in range(NY):
            aligned[y, chunk : chunk + 1] = total


def half_body(place, direct, other, out_ref):
    rows = out_ref.shape[0]
    at = pl.ds(pl.multiple_of(place[2] * rows, rows), rows)
    out_ref[...] = (direct[at] + other[at].astype(F32)).astype(BF16)


def outer_body(place, own0, own1, own2, own3, others, gains, saved, squares, out_ref, normed, left):
    tz, ty = place[0], place[1]
    width = out_ref.shape[1]
    model_width = width * BLOCKS
    gain = gains[...].astype(F32)
    per = LANES // ROWS
    for chunk in range(MICRO * BLOCKS // per):
        m, first = chunk * per // BLOCKS, chunk * per % BLOCKS
        hidden = saved[m, first * ROWS : (first + per) * ROWS].astype(F32)
        inverse = 1.0 / jnp.sqrt(squares[chunk : chunk + 1] / model_width + EPSILON)
        here = gain * hidden * columns(inverse, width)
        normed[m, first : first + per] = here.astype(BF16).reshape(per, ROWS, width)
    blocks = [(lax.rem(ty + k, NY), 0) for k in range(NY)]
    blocks += [(y, step) for y in range(NY) for step in range(1, NZ)]
    for at, (y, step) in enumerate(blocks):
        for m in range(MICRO):
            row = (at * MICRO + m) * ROWS
            left[row : row + ROWS] = normed[m, y * NZ + lax.rem(tz + step, NZ)]
    turned = jnp.transpose(left[...])
    for x in range(NX):
        at = slice(x * width, (x + 1) * width)
        mine = [ref[:, at] for ref in (own0, own1, own2, own3)]
        right = jnp.concatenate(mine + [others[y, :, at] for y in range(NY)])
        product = jnp.dot(turned, right, preferred_element_type=F32)
        out_ref[x] = (product / (MICRO * NX)).astype(BF16)


def scale_body(parts, squares, out_ref, *, model_width):
    mean = squares[...] / model_width + EPSILON
    total = parts[0] + parts[1] + parts[2] + parts[3]
    scale = total / (model_width * (mean * jnp.sqrt(mean)))
    for section in range(NS):
        out_ref[section] = scale


def fix_body(place, saved, scales, above1, above2, above3, kept, sent):
    section, core = place[3], place[2]
    chips = NS // 2
    chip = section // 2
    chip_at = [jnp.minimum(chip + d, chips - 1) for d in range(chips)]
    step = 2 * ROWS
    for m in range(MICRO):
        for first in range(0, HALF, LANES):
            line = (m * HALF + first) // LANES
            scale = []
            for d in range(chips):
                at = jnp.minimum(section + 2 * d, NS - 1)
                live = jnp.where(chip + d < chips, 1.0, 0.0)
                scale.append(scales[at, line : line + 1] * live)
            scale = jnp.transpose(jnp.concatenate(scale + scale))
            for row in range(0, LANES, step):
                at = slice(first + row, first + row + step)
                here = slice(row, row + step)
                above = above1[at].astype(F32) + above2[at].astype(F32) + above3[at].astype(F32)
                value = jnp.where(core == m, above, 0.0)
                for d in range(1, chips):
                    value = value - saved[chip_at[d], m, at].astype(F32) * scale[here, d : d + 1]
                whole = value - saved[chip, m, at].astype(F32) * scale[here, :1]
                kept[m, at] = whole
                sent[m, at] = jnp.where(core == 1, whole, value).astype(BF16)


def total_body(place, kept, got, direct, other, top, out_ref):
    use_other = jnp.where(place[2] == 0, 1.0, 0.0)
    value = top[...].astype(F32) + direct[...] + use_other * other[...].astype(F32)
    out_ref[...] = (value + (kept[...] + got[...].astype(F32))).astype(BF16)


def shards(plan, stashed, norm_gain, kv_weight, kv_grad, top_grad):
    section = lax.axis_index("section")
    core = section % 2
    index = lax.axis_index("tensor")
    tz, ty = index % NZ, index // NZ
    width = stashed.shape[-1]
    tokens = MICRO * BLOCKS * ROWS
    model_width = width * BLOCKS
    lines = tokens // LANES
    place = jnp.stack([tz, ty, core, section]).astype(jnp.int32)
    slots, weight = stashed[0], kv_weight[0]
    kvw = weight.shape[-1]
    kv0 = kv_grad.reshape(SHARE, kvw)
    half = (tokens // 2, width)

    shape = jax.ShapeDtypeStruct((NZ, SHARE, kvw + LANES), BF16)
    packed = call(pack_body, shape, [SMEM, VMEM, VMEM], (plan, kv0, slots), limit=56)
    packed, kv_y, slots = lax.optimization_barrier((packed, kv0, slots))
    kv_z = z_exchange(packed)
    own = [kv_y] + [from_y(kv_y, d) for d in (1, 2, 3)]
    hidden = jnp.where(plan[0, 0] == 0, slots, slots[::-1])
    kv_z, own, hidden = lax.optimization_barrier((kv_z, own, hidden))

    groups = [list(range(core, NS, 2)) for core in range(2)]
    saved = lax.all_gather(hidden, "section", axis_index_groups=groups)
    shape = jax.ShapeDtypeStruct((NY, (NZ - 1) * SHARE, kvw + LANES), BF16)
    others = y_exchange(call(spread_body, shape, [SMEM, VMEM], (place, kv_z)))

    flops = 2 * tokens * width * kvw
    direct, direct16, aligned, squares = call(
        back_body,
        (
            jax.ShapeDtypeStruct((tokens, width), F32),
            jax.ShapeDtypeStruct((tokens, width), BF16),
            jax.ShapeDtypeStruct((NY, lines, LANES), F32),
            jax.ShapeDtypeStruct((lines, LANES), F32),
        ),
        [SMEM] + [VMEM] * 8,
        (place, *own, others, weight, norm_gain, hidden),
        [pltpu.VMEM((MICRO, BLOCKS, ROWS, width), F32)],
        pl.CostEstimate(flops=flops, bytes_accessed=6 * 2**20, transcendentals=0),
    )
    other = from_other_core(direct16)
    aligned = jnp.sum(z_exchange(aligned), axis=0)
    other, aligned = lax.optimization_barrier((other, aligned))

    chip = call(half_body, jax.ShapeDtypeStruct(half, BF16), [SMEM, VMEM, VMEM], (place, direct, other))
    above = [from_chips_above(chip, d) for d in (1, 2, 3)]
    parts = y_exchange(jnp.broadcast_to(aligned, (NY,) + aligned.shape))
    parts, saved = lax.optimization_barrier((parts, saved))

    local = call(
        outer_body,
        jax.ShapeDtypeStruct((NX, width, width), BF16),
        [SMEM] + [VMEM] * 8,
        (place, *own, others, norm_gain, hidden, squares),
        [pltpu.VMEM((MICRO, BLOCKS, ROWS, width), BF16), pltpu.VMEM((tokens, width), BF16)],
        pl.CostEstimate(flops=flops, bytes_accessed=6 * 2**20, transcendentals=0),
    )
    weight_grads = lax.psum_scatter(local, "dp", scatter_dimension=0)[None]

    scales = call(
        functools.partial(scale_body, model_width=model_width),
        jax.ShapeDtypeStruct((NS, lines, LANES), F32),
        [VMEM, VMEM],
        (parts, squares),
    )
    scales = lax.all_to_all(scales, "section", 0, 0)
    by_micro = (MICRO, tokens // MICRO, width)
    kept, sent = call(
        fix_body,
        (jax.ShapeDtypeStruct(by_micro, F32), jax.ShapeDtypeStruct(by_micro, BF16)),
        [SMEM] + [VMEM] * 5,
        (place, saved, scales, *above),
    )
    got = from_other_core(sent)
    input_grads = call(
        total_body,
        jax.ShapeDtypeStruct(by_micro, BF16),
        [SMEM] + [VMEM] * 5,
        (place, kept, got, direct.reshape(by_micro), other.reshape(by_micro), top_grad),
    )
    return (input_grads[None], weight_grads)


def solution(mesh):
    in_specs = (
        P("section", None),
        P("section", None, "dp", "tensor"),
        P("section", "tensor"),
        P("section", "tensor", None),
        P("section", None, ("dp", "tensor"), None),
        P(None, "dp", "tensor"),
    )
    out_specs = (P("section", None, "dp", "tensor"), P("section", "tensor", "dp"))
    return jax.shard_map(shards, mesh=mesh, in_specs=in_specs, out_specs=out_specs, check_vma=False)
```

```python
import functools

import jax
import jax.numpy as jnp
from jax import lax
from jax.experimental import pallas as pl
from jax.experimental.pallas import tpu as pltpu
from jax.sharding import PartitionSpec as P

EPSILON = 1e-06
NY, NZ, NX, NS = 4, 4, 4, 8
MICRO, ROWS, LANES = 2, 16, 128
BLOCKS = NY * NZ
SHARE, HALF = MICRO * ROWS, BLOCKS * ROWS
LINES = MICRO * HALF // LANES
F32, BF16 = jnp.float32, jnp.bfloat16
VMEM = pl.BlockSpec(memory_space=pltpu.VMEM)
SMEM = pl.BlockSpec(memory_space=pltpu.SMEM)


def y_groups():
    return [[y * NZ + z for y in range(NY)] for z in range(NZ)]


def z_groups():
    return [[y * NZ + z for z in range(NZ)] for y in range(NY)]


def from_y(value, step):
    perm = [((y + step) % NY * NZ + z, y * NZ + z) for y in range(NY) for z in range(NZ)]
    return lax.ppermute(value, "tensor", perm)


def from_z(value, step):
    perm = [(y * NZ + (z + step) % NZ, y * NZ + z) for y in range(NY) for z in range(NZ)]
    return lax.ppermute(value, "tensor", perm)


def from_other_core(value):
    return lax.ppermute(value, "section", [(s, s ^ 1) for s in range(NS)])


def from_chips_above(value, chips):
    return lax.ppermute(value, "section", [(s, s - 2 * chips) for s in range(2 * chips, NS)])


def y_exchange(spread):
    return lax.all_to_all(spread, "tensor", 0, 0, axis_index_groups=y_groups())


def z_exchange(spread):
    return lax.all_to_all(spread, "tensor", 0, 0, axis_index_groups=z_groups())


def section_y_exchange(spread):
    groups = [
        [s * BLOCKS + y * NZ + z for s in range(core, NS, 2) for y in range(NY)]
        for core in range(2)
        for z in range(NZ)
    ]
    return lax.all_to_all(spread, ("section", "tensor"), 0, 0, axis_index_groups=groups)


def call(body, out_shape, specs, args, scratch=(), cost=None, limit=14):
    return pl.pallas_call(
        body,
        out_shape=out_shape,
        in_specs=specs,
        out_specs=jax.tree.map(lambda _: VMEM, out_shape),
        scratch_shapes=list(scratch),
        compiler_params=pltpu.CompilerParams(vmem_limit_bytes=limit * 2**20),
        cost_estimate=cost,
    )(*args)


def columns(row, count):
    return jnp.transpose(jnp.broadcast_to(row, (LANES, LANES)))[:, :1] + jnp.zeros((LANES, count), F32)


def parted(value):
    high = value.astype(BF16)
    rest = value - high.astype(F32)
    middle = rest.astype(BF16)
    low = (rest - middle.astype(F32)).astype(BF16)
    unused = jnp.zeros((SHARE - 3 * LINES, LANES), F32)
    stacked = [part.astype(F32) for part in (high, middle, low)]
    return jnp.concatenate(stacked + [unused]).astype(BF16)


def joined(block):
    block = block.astype(F32)
    return block[:LINES] + (block[LINES : 2 * LINES] + block[2 * LINES : 3 * LINES])


def row_sums(terms):
    folded = sum(terms[:, k * LANES : (k + 1) * LANES] for k in range(terms.shape[1] // LANES))
    return jnp.sum(jnp.transpose(folded), axis=0, keepdims=True)


def pack_body(plan, kv_ref, stashed, out_ref):
    kvw = kv_ref.shape[1]
    swap = plan[0, 0]
    sums = []
    for chunk in range(LINES):
        m, at = chunk * LANES // HALF, chunk * LANES % HALF
        hidden = stashed[m ^ swap, at : at + LANES].astype(F32)
        sums.append(row_sums(hidden * hidden))
    squares = parted(jnp.concatenate(sums))
    for z in range(NZ):
        out_ref[z, :, :kvw] = kv_ref[...]
        out_ref[z, :, kvw:] = squares


def spread_body(place, kv_ref, out_ref):
    kvw = kv_ref.shape[2] - LANES
    squares = parted(sum(joined(kv_ref[z, :, kvw:]) for z in range(NZ)))
    for step in range(1, NZ):
        block = kv_ref[lax.rem(place[0] + step, NZ), :, :kvw]
        rows = slice((step - 1) * SHARE, step * SHARE)
        for y in range(NY):
            out_ref[y, rows, :kvw] = block
            out_ref[y, rows, kvw:] = squares


def back_body(place, own0, own1, own2, own3, others, weight, gains, saved, direct, direct16, aligned, squares, grad):
    tz, ty = place[0], place[1]
    kvw = weight.shape[1]
    width = weight.shape[0]
    model_width = width * BLOCKS
    dims = (((1,), (1,)), ((), ()))
    squares[...] = sum(joined(others[y, :SHARE, kvw:]) for y in range(NY))

    def put(product, blocks):
        for at, (y, step) in enumerate(blocks):
            for m in range(MICRO):
                row = (at * MICRO + m) * ROWS
                grad[m, y * NZ + lax.rem(tz + step, NZ)] = product[row : row + ROWS]

    mine = jnp.concatenate([ref[...] for ref in (own0, own1, own2, own3)])
    product = lax.dot_general(mine, weight[...], dims, preferred_element_type=F32)
    put(product, [(lax.rem(ty + k, NY), 0) for k in range(NY)])
    rest = others[:, :, :kvw].reshape(NY * (NZ - 1) * SHARE, kvw)
    product = lax.dot_general(rest, weight[...], dims, preferred_element_type=F32)
    put(product, [(y, step) for y in range(NY) for step in range(1, NZ)])
    gain = gains[...].astype(F32)
    per = LANES // ROWS
    for chunk in range(MICRO * BLOCKS // per):
        m, first = chunk * per // BLOCKS, chunk * per % BLOCKS
        gained = grad[m, first : first + per].reshape(LANES, width) * gain
        hidden = saved[m, first * ROWS : (first + per) * ROWS].astype(F32)
        inverse = 1.0 / jnp.sqrt(squares[chunk : chunk + 1] / model_width + EPSILON)
        here = gained * columns(inverse, width)
        direct[chunk * LANES : (chunk + 1) * LANES] = here
        direct16[chunk * LANES : (chunk + 1) * LANES] = here.astype(BF16)
        mean = squares[chunk : chunk + 1] / model_width + EPSILON
        total = row_sums(gained * hidden) / (model_width * (mean * jnp.sqrt(mean)))
        for y in range(NY):
            aligned[y, chunk : chunk + 1] = total


def half_body(place, direct, other, out_ref):
    rows = out_ref.shape[0]
    at = pl.ds(pl.multiple_of(place[2] * rows, rows), rows)
    out_ref[...] = (direct[at] + other[at].astype(F32)).astype(BF16)


def outer_body(place, own0, own1, own2, own3, others, gains, saved, squares, out_ref, normed, left):
    tz, ty = place[0], place[1]
    width = out_ref.shape[1]
    model_width = width * BLOCKS
    gain = gains[...].astype(F32)
    per = LANES // ROWS
    for chunk in range(MICRO * BLOCKS // per):
        m, first = chunk * per // BLOCKS, chunk * per % BLOCKS
        hidden = saved[m, first * ROWS : (first + per) * ROWS].astype(F32)
        inverse = 1.0 / jnp.sqrt(squares[chunk : chunk + 1] / model_width + EPSILON)
        here = gain * hidden * columns(inverse, width)
        normed[m, first : first + per] = here.astype(BF16).reshape(per, ROWS, width)
    blocks = [(lax.rem(ty + k, NY), 0) for k in range(NY)]
    blocks += [(y, step) for y in range(NY) for step in range(1, NZ)]
    for at, (y, step) in enumerate(blocks):
        for m in range(MICRO):
            row = (at * MICRO + m) * ROWS
            left[row : row + ROWS] = normed[m, y * NZ + lax.rem(tz + step, NZ)]
    turned = jnp.transpose(left[...])
    for x in range(NX):
        at = slice(x * width, (x + 1) * width)
        mine = [ref[:, at] for ref in (own0, own1, own2, own3)]
        right = jnp.concatenate(mine + [others[y, :, at] for y in range(NY)])
        product = jnp.dot(turned, right, preferred_element_type=F32)
        out_ref[x] = (product / (MICRO * NX)).astype(BF16)


def fix_body(place, saved, parts, above1, above2, kept, sent):
    section, core = place[3], place[2]
    chips = NS // 2
    chip = section // 2
    chip_at = [jnp.minimum(chip + d, chips - 1) for d in range(chips)]
    step = 2 * ROWS
    for m in range(MICRO):
        for first in range(0, HALF, LANES):
            line = (m * HALF + first) // LANES
            scale = []
            for d in range(chips):
                at = jnp.minimum(chip + d, chips - 1)
                live = jnp.where(chip + d < chips, 1.0, 0.0)
                total = sum(parts[at * NY + y, line : line + 1] for y in range(NY))
                scale.append(total * live)
            scale = jnp.transpose(jnp.concatenate(scale + scale))
            for row in range(0, LANES, step):
                at = slice(first + row, first + row + step)
                here = slice(row, row + step)
                above = above1[at].astype(F32) + above2[at].astype(F32)
                value = jnp.where(core == m, above, 0.0)
                for d in range(1, chips):
                    value = value - saved[chip_at[d], m, at].astype(F32) * scale[here, d : d + 1]
                whole = value - saved[chip, m, at].astype(F32) * scale[here, :1]
                kept[m, at] = whole
                sent[m, at] = jnp.where(core == 1, whole, value).astype(BF16)


def total_body(place, kept, got, direct, other, top, out_ref):
    use_other = jnp.where(place[2] == 0, 1.0, 0.0)
    value = top[...].astype(F32) + direct[...] + use_other * other[...].astype(F32)
    out_ref[...] = (value + (kept[...] + got[...].astype(F32))).astype(BF16)


def shards(plan, stashed, norm_gain, kv_weight, kv_grad, top_grad):
    section = lax.axis_index("section")
    core = section % 2
    index = lax.axis_index("tensor")
    tz, ty = index % NZ, index // NZ
    width = stashed.shape[-1]
    tokens = MICRO * BLOCKS * ROWS
    model_width = width * BLOCKS
    lines = tokens // LANES
    place = jnp.stack([tz, ty, core, section]).astype(jnp.int32)
    slots, weight = stashed[0], kv_weight[0]
    kvw = weight.shape[-1]
    kv0 = kv_grad.reshape(SHARE, kvw)
    half = (tokens // 2, width)

    shape = jax.ShapeDtypeStruct((NZ, SHARE, kvw + LANES), BF16)
    packed = call(pack_body, shape, [SMEM, VMEM, VMEM], (plan, kv0, slots), limit=56)
    packed, kv_y, slots = lax.optimization_barrier((packed, kv0, slots))
    kv_z = z_exchange(packed)
    own = [kv_y] + [from_y(kv_y, d) for d in (1, 2, 3)]
    hidden = jnp.where(plan[0, 0] == 0, slots, slots[::-1])
    kv_z, own, hidden = lax.optimization_barrier((kv_z, own, hidden))

    groups = [list(range(core, NS, 2)) for core in range(2)]
    saved = lax.all_gather(hidden, "section", axis_index_groups=groups)
    shape = jax.ShapeDtypeStruct((NY, (NZ - 1) * SHARE, kvw + LANES), BF16)
    others = y_exchange(call(spread_body, shape, [SMEM, VMEM], (place, kv_z)))

    flops = 2 * tokens * width * kvw
    direct, direct16, aligned, squares = call(
        back_body,
        (
            jax.ShapeDtypeStruct((tokens, width), F32),
            jax.ShapeDtypeStruct((tokens, width), BF16),
            jax.ShapeDtypeStruct((NY, lines, LANES), F32),
            jax.ShapeDtypeStruct((lines, LANES), F32),
        ),
        [SMEM] + [VMEM] * 8,
        (place, *own, others, weight, norm_gain, hidden),
        [pltpu.VMEM((MICRO, BLOCKS, ROWS, width), F32)],
        pl.CostEstimate(flops=flops, bytes_accessed=6 * 2**20, transcendentals=0),
    )
    other = from_other_core(direct16)
    aligned = jnp.sum(z_exchange(aligned), axis=0)

    chip = call(half_body, jax.ShapeDtypeStruct(half, BF16), [SMEM, VMEM, VMEM], (place, direct, other))
    above1 = from_chips_above(chip, 1)
    chip, above1, aligned = lax.optimization_barrier((chip, above1, aligned))
    pair = (chip.astype(F32) + above1.astype(F32)).astype(BF16)
    above2 = from_chips_above(pair, 2)
    parts = section_y_exchange(jnp.broadcast_to(aligned, (NS // 2 * NY,) + aligned.shape))
    parts, saved = lax.optimization_barrier((parts, saved))

    local = call(
        outer_body,
        jax.ShapeDtypeStruct((NX, width, width), BF16),
        [SMEM] + [VMEM] * 8,
        (place, *own, others, norm_gain, hidden, squares),
        [pltpu.VMEM((MICRO, BLOCKS, ROWS, width), BF16), pltpu.VMEM((tokens, width), BF16)],
        pl.CostEstimate(flops=flops, bytes_accessed=6 * 2**20, transcendentals=0),
    )
    weight_grads = lax.psum_scatter(local, "dp", scatter_dimension=0)[None]

    by_micro = (MICRO, tokens // MICRO, width)
    kept, sent = call(
        fix_body,
        (jax.ShapeDtypeStruct(by_micro, F32), jax.ShapeDtypeStruct(by_micro, BF16)),
        [SMEM] + [VMEM] * 4,
        (place, saved, parts, above1, above2),
    )
    got = from_other_core(sent)
    input_grads = call(
        total_body,
        jax.ShapeDtypeStruct(by_micro, BF16),
        [SMEM] + [VMEM] * 5,
        (place, kept, got, direct.reshape(by_micro), other.reshape(by_micro), top_grad),
    )
    return (input_grads[None], weight_grads)


def solution(mesh):
    in_specs = (
        P("section", None),
        P("section", None, "dp", "tensor"),
        P("section", "tensor"),
        P("section", "tensor", None),
        P("section", None, ("dp", "tensor"), None),
        P(None, "dp", "tensor"),
    )
    out_specs = (P("section", None, "dp", "tensor"), P("section", "tensor", "dp"))
    return jax.shard_map(shards, mesh=mesh, in_specs=in_specs, out_specs=out_specs, check_vma=False)
```

```python
import functools

import jax
import jax.numpy as jnp
from jax import lax
from jax.experimental import pallas as pl
from jax.experimental.pallas import tpu as pltpu
from jax.sharding import PartitionSpec as P

EPSILON = 1e-06
NY, NZ, NX, NS = 4, 4, 4, 8
MICRO, ROWS, LANES = 2, 16, 128
BLOCKS = NY * NZ
SHARE, HALF = MICRO * ROWS, BLOCKS * ROWS
LINES = MICRO * HALF // LANES
F32, BF16 = jnp.float32, jnp.bfloat16
VMEM = pl.BlockSpec(memory_space=pltpu.VMEM)
SMEM = pl.BlockSpec(memory_space=pltpu.SMEM)


def y_groups():
    return [[y * NZ + z for y in range(NY)] for z in range(NZ)]


def z_groups():
    return [[y * NZ + z for z in range(NZ)] for y in range(NY)]


def from_y(value, step):
    perm = [((y + step) % NY * NZ + z, y * NZ + z) for y in range(NY) for z in range(NZ)]
    return lax.ppermute(value, "tensor", perm)


def from_z(value, step):
    perm = [(y * NZ + (z + step) % NZ, y * NZ + z) for y in range(NY) for z in range(NZ)]
    return lax.ppermute(value, "tensor", perm)


def from_other_core(value):
    return lax.ppermute(value, "section", [(s, s ^ 1) for s in range(NS)])


def from_chips_above(value, chips):
    return lax.ppermute(value, "section", [(s, s - 2 * chips) for s in range(2 * chips, NS)])


def y_exchange(spread):
    return lax.all_to_all(spread, "tensor", 0, 0, axis_index_groups=y_groups())


def z_exchange(spread):
    return lax.all_to_all(spread, "tensor", 0, 0, axis_index_groups=z_groups())


def section_y_exchange(spread):
    groups = [
        [s * BLOCKS + y * NZ + z for s in range(core, NS, 2) for y in range(NY)]
        for core in range(2)
        for z in range(NZ)
    ]
    return lax.all_to_all(spread, ("section", "tensor"), 0, 0, axis_index_groups=groups)


def call(body, out_shape, specs, args, scratch=(), cost=None, limit=14):
    return pl.pallas_call(
        body,
        out_shape=out_shape,
        in_specs=specs,
        out_specs=jax.tree.map(lambda _: VMEM, out_shape),
        scratch_shapes=list(scratch),
        compiler_params=pltpu.CompilerParams(vmem_limit_bytes=limit * 2**20),
        cost_estimate=cost,
    )(*args)


def columns(row, count):
    return jnp.transpose(jnp.broadcast_to(row, (LANES, LANES)))[:, :1] + jnp.zeros((LANES, count), F32)


def parted(value):
    high = value.astype(BF16)
    rest = value - high.astype(F32)
    middle = rest.astype(BF16)
    low = (rest - middle.astype(F32)).astype(BF16)
    unused = jnp.zeros((SHARE - 3 * LINES, LANES), F32)
    stacked = [part.astype(F32) for part in (high, middle, low)]
    return jnp.concatenate(stacked + [unused]).astype(BF16)


def joined(block):
    block = block.astype(F32)
    return block[:LINES] + (block[LINES : 2 * LINES] + block[2 * LINES : 3 * LINES])


def row_sums(terms):
    folded = sum(terms[:, k * LANES : (k + 1) * LANES] for k in range(terms.shape[1] // LANES))
    return jnp.sum(jnp.transpose(folded), axis=0, keepdims=True)


def pack_body(plan, kv_ref, stashed, out_ref):
    kvw = kv_ref.shape[1]
    swap = plan[0, 0]
    sums = []
    for chunk in range(LINES):
        m, at = chunk * LANES // HALF, chunk * LANES % HALF
        hidden = stashed[m ^ swap, at : at + LANES].astype(F32)
        sums.append(row_sums(hidden * hidden))
    squares = parted(jnp.concatenate(sums))
    for z in range(NZ):
        out_ref[z, :, :kvw] = kv_ref[...]
        out_ref[z, :, kvw:] = squares


def spread_body(place, kv_ref, out_ref):
    kvw = kv_ref.shape[2] - LANES
    squares = parted(sum(joined(kv_ref[z, :, kvw:]) for z in range(NZ)))
    for step in range(1, NZ):
        block = kv_ref[lax.rem(place[0] + step, NZ), :, :kvw]
        rows = slice((step - 1) * SHARE, step * SHARE)
        for y in range(NY):
            out_ref[y, rows, :kvw] = block
            out_ref[y, rows, kvw:] = squares


def back_body(place, own0, own1, own2, own3, others, weight, gains, saved, direct, direct16, aligned, squares, grad):
    tz, ty = place[0], place[1]
    kvw = weight.shape[1]
    width = weight.shape[0]
    model_width = width * BLOCKS
    dims = (((1,), (1,)), ((), ()))
    squares[...] = sum(joined(others[y, :SHARE, kvw:]) for y in range(NY))

    def put(product, blocks):
        for at, (y, step) in enumerate(blocks):
            for m in range(MICRO):
                row = (at * MICRO + m) * ROWS
                grad[m, y * NZ + lax.rem(tz + step, NZ)] = product[row : row + ROWS]

    mine = jnp.concatenate([ref[...] for ref in (own0, own1, own2, own3)])
    product = lax.dot_general(mine, weight[...], dims, preferred_element_type=F32)
    put(product, [(lax.rem(ty + k, NY), 0) for k in range(NY)])
    rest = others[:, :, :kvw].reshape(NY * (NZ - 1) * SHARE, kvw)
    product = lax.dot_general(rest, weight[...], dims, preferred_element_type=F32)
    put(product, [(y, step) for y in range(NY) for step in range(1, NZ)])
    gain = gains[...].astype(F32)
    per = LANES // ROWS
    for chunk in range(MICRO * BLOCKS // per):
        m, first = chunk * per // BLOCKS, chunk * per % BLOCKS
        gained = grad[m, first : first + per].reshape(LANES, width) * gain
        hidden = saved[m, first * ROWS : (first + per) * ROWS].astype(F32)
        inverse = 1.0 / jnp.sqrt(squares[chunk : chunk + 1] / model_width + EPSILON)
        here = gained * columns(inverse, width)
        direct[chunk * LANES : (chunk + 1) * LANES] = here
        direct16[chunk * LANES : (chunk + 1) * LANES] = here.astype(BF16)
        mean = squares[chunk : chunk + 1] / model_width + EPSILON
        total = row_sums(gained * hidden) / (model_width * (mean * jnp.sqrt(mean)))
        for y in range(NY):
            aligned[y, chunk : chunk + 1] = total


def half_body(place, direct, other, out_ref):
    rows = out_ref.shape[0]
    at = pl.ds(pl.multiple_of(place[2] * rows, rows), rows)
    out_ref[...] = (direct[at] + other[at].astype(F32)).astype(BF16)


def outer_body(place, own0, own1, own2, own3, others, gains, saved, squares, out_ref, normed, left):
    tz, ty = place[0], place[1]
    width = out_ref.shape[1]
    model_width = width * BLOCKS
    gain = gains[...].astype(F32)
    per = LANES // ROWS
    for chunk in range(MICRO * BLOCKS // per):
        m, first = chunk * per // BLOCKS, chunk * per % BLOCKS
        hidden = saved[m, first * ROWS : (first + per) * ROWS].astype(F32)
        inverse = 1.0 / jnp.sqrt(squares[chunk : chunk + 1] / model_width + EPSILON)
        here = gain * hidden * columns(inverse, width)
        normed[m, first : first + per] = here.astype(BF16).reshape(per, ROWS, width)
    blocks = [(lax.rem(ty + k, NY), 0) for k in range(NY)]
    blocks += [(y, step) for y in range(NY) for step in range(1, NZ)]
    for at, (y, step) in enumerate(blocks):
        for m in range(MICRO):
            row = (at * MICRO + m) * ROWS
            left[row : row + ROWS] = normed[m, y * NZ + lax.rem(tz + step, NZ)]
    turned = jnp.transpose(left[...])
    for x in range(NX):
        at = slice(x * width, (x + 1) * width)
        mine = [ref[:, at] for ref in (own0, own1, own2, own3)]
        right = jnp.concatenate(mine + [others[y, :, at] for y in range(NY)])
        product = jnp.dot(turned, right, preferred_element_type=F32)
        out_ref[x] = (product / (MICRO * NX)).astype(BF16)


def fix_body(place, saved, parts, above1, above2, kept, sent):
    section, core = place[3], place[2]
    chips = NS // 2
    chip = section // 2
    chip_at = [jnp.minimum(chip + d, chips - 1) for d in range(chips)]
    step = 2 * ROWS
    for m in range(MICRO):
        for first in range(0, HALF, LANES):
            line = (m * HALF + first) // LANES
            scale = []
            for d in range(chips):
                at = jnp.minimum(chip + d, chips - 1)
                live = jnp.where(chip + d < chips, 1.0, 0.0)
                total = sum(parts[at * NY + y, line : line + 1] for y in range(NY))
                scale.append(total * live)
            scale = jnp.transpose(jnp.concatenate(scale + scale))
            for row in range(0, LANES, step):
                at = slice(first + row, first + row + step)
                here = slice(row, row + step)
                above = above1[at].astype(F32) + above2[at].astype(F32)
                value = jnp.where(core == m, above, 0.0)
                for d in range(1, chips):
                    value = value - saved[chip_at[d], m, at].astype(F32) * scale[here, d : d + 1]
                whole = value - saved[chip, m, at].astype(F32) * scale[here, :1]
                kept[m, at] = whole
                sent[m, at] = jnp.where(core == 1, whole, value).astype(BF16)


def total_body(place, kept, got, direct, other, top, out_ref):
    use_other = jnp.where(place[2] == 0, 1.0, 0.0)
    value = top[...].astype(F32) + direct[...] + use_other * other[...].astype(F32)
    out_ref[...] = (value + (kept[...] + got[...].astype(F32))).astype(BF16)


def shards(plan, stashed, norm_gain, kv_weight, kv_grad, top_grad):
    section = lax.axis_index("section")
    core = section % 2
    index = lax.axis_index("tensor")
    tz, ty = index % NZ, index // NZ
    width = stashed.shape[-1]
    tokens = MICRO * BLOCKS * ROWS
    model_width = width * BLOCKS
    lines = tokens // LANES
    place = jnp.stack([tz, ty, core, section]).astype(jnp.int32)
    slots, weight = stashed[0], kv_weight[0]
    kvw = weight.shape[-1]
    kv0 = kv_grad.reshape(SHARE, kvw)
    half = (tokens // 2, width)

    shape = jax.ShapeDtypeStruct((NZ, SHARE, kvw + LANES), BF16)
    packed = call(pack_body, shape, [SMEM, VMEM, VMEM], (plan, kv0, slots), limit=56)
    packed, kv_y, slots = lax.optimization_barrier((packed, kv0, slots))
    kv_z = z_exchange(packed)
    own = [kv_y] + [from_y(kv_y, d) for d in (1, 2, 3)]
    hidden = jnp.where(plan[0, 0] == 0, slots, slots[::-1])
    kv_z, own, hidden = lax.optimization_barrier((kv_z, own, hidden))

    groups = [list(range(core, NS, 2)) for core in range(2)]
    saved = lax.all_gather(hidden, "section", axis_index_groups=groups)
    shape = jax.ShapeDtypeStruct((NY, (NZ - 1) * SHARE, kvw + LANES), BF16)
    others = y_exchange(call(spread_body, shape, [SMEM, VMEM], (place, kv_z)))

    flops = 2 * tokens * width * kvw
    direct, direct16, aligned, squares = call(
        back_body,
        (
            jax.ShapeDtypeStruct((tokens, width), F32),
            jax.ShapeDtypeStruct((tokens, width), BF16),
            jax.ShapeDtypeStruct((NY, lines, LANES), F32),
            jax.ShapeDtypeStruct((lines, LANES), F32),
        ),
        [SMEM] + [VMEM] * 8,
        (place, *own, others, weight, norm_gain, hidden),
        [pltpu.VMEM((MICRO, BLOCKS, ROWS, width), F32)],
        pl.CostEstimate(flops=flops, bytes_accessed=6 * 2**20, transcendentals=0),
    )
    other = from_other_core(direct16)
    aligned = jnp.sum(z_exchange(aligned), axis=0)

    chip = call(half_body, jax.ShapeDtypeStruct(half, BF16), [SMEM, VMEM, VMEM], (place, direct, other))
    above1 = from_chips_above(chip, 1)
    chip, above1, aligned = lax.optimization_barrier((chip, above1, aligned))
    pair = (chip.astype(F32) + above1.astype(F32)).astype(BF16)
    above2 = from_chips_above(pair, 2)
    aligned, saved = lax.optimization_barrier((aligned, saved))
    parts = section_y_exchange(jnp.broadcast_to(aligned, (NS // 2 * NY,) + aligned.shape))

    local = call(
        outer_body,
        jax.ShapeDtypeStruct((NX, width, width), BF16),
        [SMEM] + [VMEM] * 8,
        (place, *own, others, norm_gain, hidden, squares),
        [pltpu.VMEM((MICRO, BLOCKS, ROWS, width), BF16), pltpu.VMEM((tokens, width), BF16)],
        pl.CostEstimate(flops=flops, bytes_accessed=6 * 2**20, transcendentals=0),
    )
    weight_grads = lax.psum_scatter(local, "dp", scatter_dimension=0)[None]

    by_micro = (MICRO, tokens // MICRO, width)
    kept, sent = call(
        fix_body,
        (jax.ShapeDtypeStruct(by_micro, F32), jax.ShapeDtypeStruct(by_micro, BF16)),
        [SMEM] + [VMEM] * 4,
        (place, saved, parts, above1, above2),
    )
    got = from_other_core(sent)
    input_grads = call(
        total_body,
        jax.ShapeDtypeStruct(by_micro, BF16),
        [SMEM] + [VMEM] * 5,
        (place, kept, got, direct.reshape(by_micro), other.reshape(by_micro), top_grad),
    )
    return (input_grads[None], weight_grads)


def solution(mesh):
    in_specs = (
        P("section", None),
        P("section", None, "dp", "tensor"),
        P("section", "tensor"),
        P("section", "tensor", None),
        P("section", None, ("dp", "tensor"), None),
        P(None, "dp", "tensor"),
    )
    out_specs = (P("section", None, "dp", "tensor"), P("section", "tensor", "dp"))
    return jax.shard_map(shards, mesh=mesh, in_specs=in_specs, out_specs=out_specs, check_vma=False)
```

```python
import functools

import jax
import jax.numpy as jnp
from jax import lax
from jax.experimental import pallas as pl
from jax.experimental.pallas import tpu as pltpu
from jax.sharding import PartitionSpec as P

EPSILON = 1e-06
NY, NZ, NX, NS = 4, 4, 4, 8
MICRO, ROWS, LANES = 2, 16, 128
BLOCKS = NY * NZ
SHARE, HALF = MICRO * ROWS, BLOCKS * ROWS
LINES = MICRO * HALF // LANES
F32, BF16 = jnp.float32, jnp.bfloat16
VMEM = pl.BlockSpec(memory_space=pltpu.VMEM)
SMEM = pl.BlockSpec(memory_space=pltpu.SMEM)


def y_groups():
    return [[y * NZ + z for y in range(NY)] for z in range(NZ)]


def z_groups():
    return [[y * NZ + z for z in range(NZ)] for y in range(NY)]


def from_y(value, step):
    perm = [((y + step) % NY * NZ + z, y * NZ + z) for y in range(NY) for z in range(NZ)]
    return lax.ppermute(value, "tensor", perm)


def from_z(value, step):
    perm = [(y * NZ + (z + step) % NZ, y * NZ + z) for y in range(NY) for z in range(NZ)]
    return lax.ppermute(value, "tensor", perm)


def from_other_core(value):
    return lax.ppermute(value, "section", [(s, s ^ 1) for s in range(NS)])


def from_chips_above(value, chips):
    return lax.ppermute(value, "section", [(s, s - 2 * chips) for s in range(2 * chips, NS)])


def y_exchange(spread):
    return lax.all_to_all(spread, "tensor", 0, 0, axis_index_groups=y_groups())


def z_exchange(spread):
    return lax.all_to_all(spread, "tensor", 0, 0, axis_index_groups=z_groups())


def section_y_exchange(spread):
    groups = [
        [s * BLOCKS + y * NZ + z for s in range(core, NS, 2) for y in range(NY)]
        for core in range(2)
        for z in range(NZ)
    ]
    return lax.all_to_all(spread, ("section", "tensor"), 0, 0, axis_index_groups=groups)


def call(body, out_shape, specs, args, scratch=(), cost=None, limit=14):
    return pl.pallas_call(
        body,
        out_shape=out_shape,
        in_specs=specs,
        out_specs=jax.tree.map(lambda _: VMEM, out_shape),
        scratch_shapes=list(scratch),
        compiler_params=pltpu.CompilerParams(vmem_limit_bytes=limit * 2**20),
        cost_estimate=cost,
    )(*args)


def columns(row, count):
    return jnp.transpose(jnp.broadcast_to(row, (LANES, LANES)))[:, :1] + jnp.zeros((LANES, count), F32)


def parted(value):
    high = value.astype(BF16)
    rest = value - high.astype(F32)
    middle = rest.astype(BF16)
    low = (rest - middle.astype(F32)).astype(BF16)
    unused = jnp.zeros((SHARE - 3 * LINES, LANES), F32)
    stacked = [part.astype(F32) for part in (high, middle, low)]
    return jnp.concatenate(stacked + [unused]).astype(BF16)


def joined(block):
    block = block.astype(F32)
    return block[:LINES] + (block[LINES : 2 * LINES] + block[2 * LINES : 3 * LINES])


def row_sums(terms):
    folded = sum(terms[:, k * LANES : (k + 1) * LANES] for k in range(terms.shape[1] // LANES))
    return jnp.sum(jnp.transpose(folded), axis=0, keepdims=True)


def pack_body(plan, kv_ref, stashed, out_ref):
    kvw = kv_ref.shape[1]
    swap = plan[0, 0]
    sums = []
    for chunk in range(LINES):
        m, at = chunk * LANES // HALF, chunk * LANES % HALF
        hidden = stashed[m ^ swap, at : at + LANES].astype(F32)
        sums.append(row_sums(hidden * hidden))
    squares = parted(jnp.concatenate(sums))
    for z in range(NZ):
        out_ref[z, :, :kvw] = kv_ref[...]
        out_ref[z, :, kvw:] = squares


def spread_body(place, kv_ref, out_ref):
    kvw = kv_ref.shape[2] - LANES
    squares = parted(sum(joined(kv_ref[z, :, kvw:]) for z in range(NZ)))
    for step in range(1, NZ):
        block = kv_ref[lax.rem(place[0] + step, NZ), :, :kvw]
        rows = slice((step - 1) * SHARE, step * SHARE)
        for y in range(NY):
            out_ref[y, rows, :kvw] = block
            out_ref[y, rows, kvw:] = squares


def back_body(place, own0, own1, own2, own3, others, weight, gains, saved, direct, direct16, aligned, squares, grad):
    tz, ty = place[0], place[1]
    kvw = weight.shape[1]
    width = weight.shape[0]
    model_width = width * BLOCKS
    dims = (((1,), (1,)), ((), ()))
    squares[...] = sum(joined(others[y, :SHARE, kvw:]) for y in range(NY))

    def put(product, blocks):
        for at, (y, step) in enumerate(blocks):
            for m in range(MICRO):
                row = (at * MICRO + m) * ROWS
                grad[m, y * NZ + lax.rem(tz + step, NZ)] = product[row : row + ROWS]

    mine = jnp.concatenate([ref[...] for ref in (own0, own1, own2, own3)])
    product = lax.dot_general(mine, weight[...], dims, preferred_element_type=F32)
    put(product, [(lax.rem(ty + k, NY), 0) for k in range(NY)])
    rest = others[:, :, :kvw].reshape(NY * (NZ - 1) * SHARE, kvw)
    product = lax.dot_general(rest, weight[...], dims, preferred_element_type=F32)
    put(product, [(y, step) for y in range(NY) for step in range(1, NZ)])
    gain = gains[...].astype(F32)
    per = LANES // ROWS
    for chunk in range(MICRO * BLOCKS // per):
        m, first = chunk * per // BLOCKS, chunk * per % BLOCKS
        gained = grad[m, first : first + per].reshape(LANES, width) * gain
        hidden = saved[m, first * ROWS : (first + per) * ROWS].astype(F32)
        inverse = 1.0 / jnp.sqrt(squares[chunk : chunk + 1] / model_width + EPSILON)
        here = gained * columns(inverse, width)
        direct[chunk * LANES : (chunk + 1) * LANES] = here
        direct16[chunk * LANES : (chunk + 1) * LANES] = here.astype(BF16)
        mean = squares[chunk : chunk + 1] / model_width + EPSILON
        total = row_sums(gained * hidden) / (model_width * (mean * jnp.sqrt(mean)))
        for y in range(NY):
            aligned[y, chunk : chunk + 1] = total


def half_body(place, direct, other, out_ref):
    rows = out_ref.shape[0]
    at = pl.ds(pl.multiple_of(place[2] * rows, rows), rows)
    out_ref[...] = (direct[at] + other[at].astype(F32)).astype(BF16)


def outer_body(place, own0, own1, own2, own3, others, gains, saved, squares, out_ref, normed, left):
    tz, ty = place[0], place[1]
    width = out_ref.shape[1]
    model_width = width * BLOCKS
    gain = gains[...].astype(F32)
    per = LANES // ROWS
    for chunk in range(MICRO * BLOCKS // per):
        m, first = chunk * per // BLOCKS, chunk * per % BLOCKS
        hidden = saved[m, first * ROWS : (first + per) * ROWS].astype(F32)
        inverse = 1.0 / jnp.sqrt(squares[chunk : chunk + 1] / model_width + EPSILON)
        here = gain * hidden * columns(inverse, width)
        normed[m, first : first + per] = here.astype(BF16).reshape(per, ROWS, width)
    blocks = [(lax.rem(ty + k, NY), 0) for k in range(NY)]
    blocks += [(y, step) for y in range(NY) for step in range(1, NZ)]
    for at, (y, step) in enumerate(blocks):
        for m in range(MICRO):
            row = (at * MICRO + m) * ROWS
            left[row : row + ROWS] = normed[m, y * NZ + lax.rem(tz + step, NZ)]
    turned = jnp.transpose(left[...])
    for x in range(NX):
        at = slice(x * width, (x + 1) * width)
        mine = [ref[:, at] for ref in (own0, own1, own2, own3)]
        right = jnp.concatenate(mine + [others[y, :, at] for y in range(NY)])
        product = jnp.dot(turned, right, preferred_element_type=F32)
        out_ref[x] = (product / (MICRO * NX)).astype(BF16)


def order_body(place, saved, out_ref):
    chip, chips = place[3] // 2, saved.shape[0]
    for d in range(chips):
        out_ref[d] = saved[jnp.minimum(chip + d, chips - 1)]


def fix_body(place, saved, parts, above1, above2, kept, sent):
    section, core = place[3], place[2]
    chips = NS // 2
    chip = section // 2
    step = 2 * ROWS
    for m in range(MICRO):
        for first in range(0, HALF, LANES):
            line = (m * HALF + first) // LANES
            scale = []
            for d in range(chips):
                at = jnp.minimum(chip + d, chips - 1)
                live = jnp.where(chip + d < chips, 1.0, 0.0)
                total = sum(parts[at * NY + y, line : line + 1] for y in range(NY))
                scale.append(total * live)
            scale = jnp.transpose(jnp.concatenate(scale + scale))
            for row in range(0, LANES, step):
                at = slice(first + row, first + row + step)
                here = slice(row, row + step)
                above = above1[at].astype(F32) + above2[at].astype(F32)
                value = jnp.where(core == m, above, 0.0)
                for d in range(1, chips):
                    value = value - saved[d, m, at].astype(F32) * scale[here, d : d + 1]
                whole = value - saved[0, m, at].astype(F32) * scale[here, :1]
                kept[m, at] = whole
                sent[m, at] = jnp.where(core == 1, whole, value).astype(BF16)


def total_body(place, kept, got, direct, other, top, out_ref):
    use_other = jnp.where(place[2] == 0, 1.0, 0.0)
    value = top[...].astype(F32) + direct[...] + use_other * other[...].astype(F32)
    out_ref[...] = (value + (kept[...] + got[...].astype(F32))).astype(BF16)


def shards(plan, stashed, norm_gain, kv_weight, kv_grad, top_grad):
    section = lax.axis_index("section")
    core = section % 2
    index = lax.axis_index("tensor")
    tz, ty = index % NZ, index // NZ
    width = stashed.shape[-1]
    tokens = MICRO * BLOCKS * ROWS
    model_width = width * BLOCKS
    lines = tokens // LANES
    place = jnp.stack([tz, ty, core, section]).astype(jnp.int32)
    slots, weight = stashed[0], kv_weight[0]
    kvw = weight.shape[-1]
    kv0 = kv_grad.reshape(SHARE, kvw)
    half = (tokens // 2, width)

    shape = jax.ShapeDtypeStruct((NZ, SHARE, kvw + LANES), BF16)
    packed = call(pack_body, shape, [SMEM, VMEM, VMEM], (plan, kv0, slots), limit=56)
    packed, kv_y, slots = lax.optimization_barrier((packed, kv0, slots))
    kv_z = z_exchange(packed)
    own = [kv_y] + [from_y(kv_y, d) for d in (1, 2, 3)]
    hidden = jnp.where(plan[0, 0] == 0, slots, slots[::-1])
    kv_z, own, hidden = lax.optimization_barrier((kv_z, own, hidden))

    groups = [list(range(core, NS, 2)) for core in range(2)]
    saved = lax.all_gather(hidden, "section", axis_index_groups=groups)
    shape = jax.ShapeDtypeStruct((NY, (NZ - 1) * SHARE, kvw + LANES), BF16)
    others = y_exchange(call(spread_body, shape, [SMEM, VMEM], (place, kv_z)))

    flops = 2 * tokens * width * kvw
    direct, direct16, aligned, squares = call(
        back_body,
        (
            jax.ShapeDtypeStruct((tokens, width), F32),
            jax.ShapeDtypeStruct((tokens, width), BF16),
            jax.ShapeDtypeStruct((NY, lines, LANES), F32),
            jax.ShapeDtypeStruct((lines, LANES), F32),
        ),
        [SMEM] + [VMEM] * 8,
        (place, *own, others, weight, norm_gain, hidden),
        [pltpu.VMEM((MICRO, BLOCKS, ROWS, width), F32)],
        pl.CostEstimate(flops=flops, bytes_accessed=6 * 2**20, transcendentals=0),
    )
    other = from_other_core(direct16)
    aligned = jnp.sum(z_exchange(aligned), axis=0)

    chip = call(half_body, jax.ShapeDtypeStruct(half, BF16), [SMEM, VMEM, VMEM], (place, direct, other))
    above1 = from_chips_above(chip, 1)
    chip, above1, aligned = lax.optimization_barrier((chip, above1, aligned))
    pair = (chip.astype(F32) + above1.astype(F32)).astype(BF16)
    above2 = from_chips_above(pair, 2)
    aligned, saved = lax.optimization_barrier((aligned, saved))
    parts = section_y_exchange(jnp.broadcast_to(aligned, (NS // 2 * NY,) + aligned.shape))

    local = call(
        outer_body,
        jax.ShapeDtypeStruct((NX, width, width), BF16),
        [SMEM] + [VMEM] * 8,
        (place, *own, others, norm_gain, hidden, squares),
        [pltpu.VMEM((MICRO, BLOCKS, ROWS, width), BF16), pltpu.VMEM((tokens, width), BF16)],
        pl.CostEstimate(flops=flops, bytes_accessed=6 * 2**20, transcendentals=0),
    )
    weight_grads = lax.psum_scatter(local, "dp", scatter_dimension=0)[None]

    by_micro = (MICRO, tokens // MICRO, width)
    saved = call(order_body, jax.ShapeDtypeStruct(saved.shape, BF16), [SMEM, VMEM], (place, saved))
    kept, sent = call(
        fix_body,
        (jax.ShapeDtypeStruct(by_micro, F32), jax.ShapeDtypeStruct(by_micro, BF16)),
        [SMEM] + [VMEM] * 4,
        (place, saved, parts, above1, above2),
    )
    got = from_other_core(sent)
    input_grads = call(
        total_body,
        jax.ShapeDtypeStruct(by_micro, BF16),
        [SMEM] + [VMEM] * 5,
        (place, kept, got, direct.reshape(by_micro), other.reshape(by_micro), top_grad),
    )
    return (input_grads[None], weight_grads)


def solution(mesh):
    in_specs = (
        P("section", None),
        P("section", None, "dp", "tensor"),
        P("section", "tensor"),
        P("section", "tensor", None),
        P("section", None, ("dp", "tensor"), None),
        P(None, "dp", "tensor"),
    )
    out_specs = (P("section", None, "dp", "tensor"), P("section", "tensor", "dp"))
    return jax.shard_map(shards, mesh=mesh, in_specs=in_specs, out_specs=out_specs, check_vma=False)
```
